32 devices in a mesh: grp: 2 (over y), rot: 4 (over z), shell: 2 (over x), ang: 2 (over core).
Axes of the slice: x: 2, y: 2, z: 4, core: 2. Of those that a mesh axis runs over, the one named last changes fastest.
Arguments:
- images: float32 [2, 128, 64, 2048], P(None, 'shell', 'ang', ('grp', 'rot')), parts along dimension 3, may hold values from -16 to 16
- references: bfloat16 [2, 128, 64, 2048], P(None, 'shell', 'ang', ('grp', 'rot')), parts along dimension 3, may hold values from -4 to 4
- noise_weight: float32 [256], P(('grp', 'shell')), parts along dimension 0, may hold values from 0.004 to 0.03
- euler_angles: float32 [3, 2048], P(None, ('grp', 'rot')), parts along dimension 1, may hold values from -3.140625 to 3.140625
- candidate_count: int32 [16, 4], P(('grp', 'rot')), parts along dimension 0, may hold values from 0 to 8, as said below
- candidate_rotation: int32 [16, 4, 8], P(('grp', 'rot')), parts along dimension 0, may hold values from 0 to 255, as said below
- image_order: int32 [2048], P(('grp', 'rot')), parts along dimension 0, may hold values from 0 to 255, as said below
Outputs:
- coefficients: float32 [2048, 2, 128], P(('grp', 'rot', 'ang'), None, 'shell'), parts along dimension 0
- log_evidence: float32 [2048], P(('grp', 'rot')), parts along dimension 0
The draws below stay inside these ranges and needn't reach their ends.
There are 2 independent parts, one for each index of `grp`. The reference program is written for one: setup_inputs(seed, part) draws one part's arguments, and reference() takes and returns one part's arrays. A program takes and returns all parts, laid end to end along the dimension named above; each array names one. Nothing has to cross between parts.
Inputs may be any that keep to these rules, and one draw needn't show every extreme that they name: `image_order`: within each device's 256 entries, a permutation of 0 to 255. `candidate_count`: for the 2 blocks of one device and one owner the counts add up to at most 8; in every draw one owner, drawn from the seed, gets exactly 8 from every device, with 8 in one block of each device; every block has two or more candidates in all. `candidate_rotation`: the 8 entries of one block and owner are distinct; entries at or past the count are not used.
All inputs are finite; a program needn't handle non-finite values.
Results may differ from the reference program's by a relative error of at most 0.0074.
Values may be sent and summed in bfloat16 or wider, within the bound.
A program may use at most 64 MiB of HBM per device.

```python
import math
import jax
import jax.numpy as jnp
from jax import lax

SHELLS = 128
ANGLES = 64
ORDER = 32
BLOCK = 128
CPO = 8
IMG_DEV = 256
ROT_DEV = 256
COEF = 1024
BLK_DEV = 2
OWNERS = 4
IMAGES = 1024
BLOCKS = 8
ROTS = 1024


def permute_one(shuffle_key):
    return jax.random.permutation(shuffle_key, IMG_DEV)


def shared_draw(key):
    subkeys = jax.random.split(jax.random.fold_in(key, 4099), 9)
    references = jnp.clip(jax.random.normal(subkeys[0], (2, SHELLS, ANGLES, ROTS), jnp.float32), -4.0, 4.0)
    noise_weight = jnp.exp(jax.random.uniform(subkeys[2], (SHELLS,), jnp.float32, math.log(0.004), math.log(0.03)))
    popular = jax.random.randint(subkeys[3], (OWNERS,), 0, 4)
    raw_draw = jax.random.randint(subkeys[4], (OWNERS, BLK_DEV, OWNERS), 0, CPO // 2)
    counts = jnp.minimum(CPO // 2, 1 + raw_draw * popular[None, None, :] // 2)
    forced_owner = jax.random.randint(subkeys[5], (), 0, OWNERS)
    forced_block = jax.random.randint(subkeys[6], (OWNERS,), 0, BLK_DEV)
    block_rank = (jnp.arange(BLK_DEV)[None, :] - forced_block[:, None]) % BLK_DEV
    forced_counts = jnp.where(block_rank == 0, CPO, jnp.where(block_rank <= BLK_DEV - 2, CPO // 2, 0))
    forced_mask = (jnp.arange(OWNERS) == forced_owner)[None, None, :]
    counts = jnp.where(forced_mask, forced_counts[:, :, None], counts).reshape(BLOCKS, OWNERS).astype(jnp.int32)
    scores = jax.random.randint(subkeys[7], (BLOCKS, OWNERS, ROT_DEV), 0, 1 << 20) * ROT_DEV + jnp.arange(ROT_DEV)
    indices = lax.top_k(scores.astype(jnp.int32), CPO)[1].astype(jnp.int32)
    shuffle_keys = jax.random.split(subkeys[8], OWNERS)
    ordering = jax.vmap(permute_one)(shuffle_keys).reshape(IMAGES).astype(jnp.int32)
    return (references, noise_weight, counts, indices, ordering)


def draw_references(key, part):
    return shared_draw(key)[0].astype(jnp.bfloat16)


def draw_noise_weight(key, part):
    return shared_draw(key)[1]


def draw_candidate_count(key, part):
    return shared_draw(key)[2]


def draw_candidate_rotation(key, part):
    return shared_draw(key)[3]


def draw_image_order(key, part):
    return shared_draw(key)[4]


def draw_images(key, part):
    subkeys = jax.random.split(jax.random.fold_in(key, 7919), 3)
    return jnp.clip(jax.random.normal(subkeys[2], (2, SHELLS, ANGLES, IMAGES), jnp.float32), -6.0, 6.0)


def setup_inputs(seed: int = 0, part: int = 0) -> dict:
    arg_keys = jax.random.split(jax.random.key(seed), 8)
    own_keys = jax.random.split(jax.random.fold_in(arg_keys[7], part), 8)
    images = draw_images(jax.random.fold_in(jax.random.fold_in(arg_keys[7], part), 71), part)
    references = draw_references(jax.random.fold_in(jax.random.fold_in(arg_keys[7], part), 71), part)
    noise_weight = draw_noise_weight(jax.random.fold_in(jax.random.fold_in(arg_keys[7], part), 71), part)
    euler_angles = jnp.clip(jax.random.uniform(own_keys[3], (3, ROTS), jnp.float32, -3.140625, 3.140625), -3.140625, 3.140625)
    candidate_count = draw_candidate_count(jax.random.fold_in(jax.random.fold_in(arg_keys[7], part), 71), part)
    candidate_rotation = draw_candidate_rotation(jax.random.fold_in(jax.random.fold_in(arg_keys[7], part), 71), part)
    image_order = draw_image_order(jax.random.fold_in(jax.random.fold_in(arg_keys[7], part), 71), part)
    return {"images": images, "references": references, "noise_weight": noise_weight, "euler_angles": euler_angles, "candidate_count": candidate_count, "candidate_rotation": candidate_rotation, "image_order": image_order}


def legendre_constants(degrees):
    first_coef = []
    second_coef = []
    for degree in range(degrees):
        first_line = []
        second_line = []
        for azimuth in range(degrees):
            if azimuth < degree:
                first_line.append(math.sqrt((4.0 * degree * degree - 1.0) / (degree * degree - azimuth * azimuth)))
                lower_term = max((degree - 1.0) ** 2 - azimuth * azimuth, 0.0)
                lower_den = max(4.0 * (degree - 1.0) ** 2 - 1.0, 1.0)
                second_line.append(math.sqrt(lower_term / lower_den))
            else:
                first_line.append(0.0)
                second_line.append(0.0)
        first_coef.append(first_line)
        second_coef.append(second_line)
    diagonal = []
    running = 1.0
    for degree in range(degrees):
        if degree > 0:
            running = running * (2.0 * degree - 1.0) / (2.0 * degree)
        diagonal.append(math.sqrt((2.0 * degree + 1.0) / (4.0 * math.pi) * running))
    pick_rows = []
    pick_trig = []
    factors = []
    for degree in range(degrees):
        pick_rows.append(degree * degrees)
        pick_trig.append(0)
        factors.append(1.0)
        for azimuth in range(1, degree + 1):
            for parity in range(2):
                pick_rows.append(degree * degrees + azimuth)
                pick_trig.append(parity * degrees + azimuth)
                factors.append(math.sqrt(2.0))
    return (first_coef, second_coef, diagonal, pick_rows, pick_trig, factors)

def harmonic_table(euler_angles, angle_ids, angle_count, degrees):
    first_coef, second_coef, diagonal, pick_rows, pick_trig, factors = legendre_constants(degrees)
    in_plane = 2.0 * math.pi / angle_count * angle_ids.astype(jnp.float32)
    phases = in_plane[:, None] + euler_angles[2][None, :]
    cos_phase = jnp.cos(phases)
    sin_phase = jnp.sin(phases)
    cos_alpha = jnp.cos(euler_angles[0])[None, :]
    sin_alpha = jnp.sin(euler_angles[0])[None, :]
    cos_beta = jnp.cos(euler_angles[1])[None, :]
    sin_beta = jnp.sin(euler_angles[1])[None, :]
    along_x = (cos_alpha * cos_beta * cos_phase - sin_alpha * sin_phase).reshape(-1)
    along_y = (sin_alpha * cos_beta * cos_phase + cos_alpha * sin_phase).reshape(-1)
    along_z = (-sin_beta * cos_phase).reshape(-1)

    def trig_step(carry, unused):
        real_part, imag_part = carry
        return ((along_x * real_part - along_y * imag_part, along_x * imag_part + along_y * real_part), carry)
    unused_carry, (real_rows, imag_rows) = lax.scan(trig_step, (jnp.ones_like(along_x), jnp.zeros_like(along_x)), None, length=degrees)
    azimuths = jnp.arange(degrees)
    diag_col = jnp.asarray(diagonal, jnp.float32)[:, None]

    def legendre_step(carry, inputs):
        previous, earlier = carry
        degree, coef_first, coef_second = inputs
        current = coef_first[:, None] * (along_z[None, :] * previous - coef_second[:, None] * earlier)
        current = jnp.where((azimuths == degree)[:, None], diag_col, current)
        return ((current, previous), current)
    zero_rows = jnp.zeros((degrees, along_z.shape[0]), jnp.float32)
    unused_state, stacked = lax.scan(legendre_step, (zero_rows, zero_rows), (jnp.arange(degrees), jnp.asarray(first_coef, jnp.float32), jnp.asarray(second_coef, jnp.float32)))
    legendre = stacked.reshape(degrees * degrees, -1)
    trig_rows = jnp.concatenate([real_rows, imag_rows], axis=0)
    table_rows = jnp.take(legendre, jnp.asarray(pick_rows, jnp.int32), axis=0) * jnp.take(trig_rows, jnp.asarray(pick_trig, jnp.int32), axis=0) * jnp.asarray(factors, jnp.float32)[:, None]
    return table_rows.astype(jnp.bfloat16)

def reference(images, references, noise_weight, euler_angles, candidate_count, candidate_rotation, image_order):
    features = 2 * SHELLS * ANGLES
    shell_scale = jnp.broadcast_to(noise_weight[None, :, None], (2, SHELLS, ANGLES)).reshape(features)
    weighted = (images.reshape(features, IMAGES) * shell_scale[:, None]).astype(jnp.bfloat16)
    slice_table = references.reshape(features, ROTS)
    slot_ids = jnp.arange(CPO)
    owner_ids = jnp.arange(OWNERS)

    def one_block(running_sum, block_id):
        first_pos = block_id * BLOCK
        device = first_pos // IMG_DEV
        members = device * IMG_DEV + lax.dynamic_slice_in_dim(image_order, first_pos, BLOCK)
        columns = jnp.take(weighted, members, axis=1).astype(jnp.float32)
        rotation_ids = (owner_ids[:, None] * ROT_DEV + candidate_rotation[block_id]).reshape(-1)
        is_valid = (slot_ids[None, :] < candidate_count[block_id][:, None]).reshape(-1)
        slices = jnp.take(slice_table, rotation_ids, axis=1).astype(jnp.float32)
        slot_norms = lax.optimization_barrier(jnp.sum(jnp.square(slices) * shell_scale[:, None], axis=0))
        scores = 2.0 * lax.dot_general(columns, slices, (((0,), (0,)), ((), ())), precision=lax.Precision.HIGHEST, preferred_element_type=jnp.float32) - slot_norms[None, :]
        masked = jnp.where(is_valid[None, :], scores, -jnp.inf)
        highest = lax.optimization_barrier(jnp.max(masked, axis=1))
        totals = lax.optimization_barrier(jnp.sum(jnp.exp(masked - highest[:, None]), axis=1))
        evidence = highest + jnp.log(totals)
        weights = jnp.exp(masked - evidence[:, None]).astype(jnp.bfloat16).astype(jnp.float32)
        averages = jnp.dot(columns, weights, precision=lax.Precision.HIGHEST, preferred_element_type=jnp.float32).astype(jnp.bfloat16)
        running_sum = running_sum.at[:, rotation_ids].add(averages.astype(jnp.float32))
        return (running_sum, evidence)
    running_sum, evidence = lax.scan(one_block, jnp.zeros((features, ROTS), jnp.float32), jnp.arange(BLOCKS).astype(jnp.int32))
    positions = jnp.arange(IMAGES)
    image_ids = positions // IMG_DEV * IMG_DEV + image_order
    log_evidence = jnp.zeros((IMAGES,), jnp.float32).at[image_ids].set(evidence.reshape(-1))
    rotation_average = running_sum.astype(jnp.bfloat16).reshape(2 * SHELLS, ANGLES, ROTS)

    def one_angle(coef_sum, angle_id):
        harmonics = harmonic_table(euler_angles, angle_id[None], ANGLES, ORDER).astype(jnp.float32)
        angle_plane = lax.dynamic_index_in_dim(rotation_average, angle_id, 1, keepdims=False).astype(jnp.float32)
        return (coef_sum + lax.dot_general(harmonics, angle_plane, (((1,), (1,)), ((), ())), precision=lax.Precision.HIGHEST, preferred_element_type=jnp.float32), None)
    coefficients, unused = lax.scan(one_angle, jnp.zeros((COEF, 2 * SHELLS), jnp.float32), jnp.arange(ANGLES).astype(jnp.int32))
    return (coefficients.reshape(COEF, 2, SHELLS), log_evidence)
```

```python
import functools
import math

import jax
import jax.numpy as jnp
import numpy as np
from jax import lax
from jax.experimental import pallas as pl
from jax.experimental.pallas import tpu as pltpu
from jax.sharding import PartitionSpec as P

ANGLES = 64
ORDER = 32
BLOCK = 128
CPO = 8
COEF = 1024
HALF = 16
ROWS = 2 * HALF * HALF + 2 * (ORDER - HALF) * ORDER
LANES = 128
CHUNK = 256
MESH = pl.DeviceIdType.MESH


def legendre_constants(degrees):
    table = np.zeros((degrees, 2 * degrees), np.float32)
    diagonal = []
    running = 1.0
    for degree in range(degrees):
        for azimuth in range(degree):
            table[azimuth, degree] = math.sqrt(
                (4.0 * degree * degree - 1.0) / (degree * degree - azimuth * azimuth)
            )
            lower_term = max((degree - 1.0) ** 2 - azimuth * azimuth, 0.0)
            lower_den = max(4.0 * (degree - 1.0) ** 2 - 1.0, 1.0)
            table[azimuth, degrees + degree] = math.sqrt(lower_term / lower_den)
        if degree > 0:
            running = running * (2.0 * degree - 1.0) / (2.0 * degree)
        diagonal.append(math.sqrt((2.0 * degree + 1.0) / (4.0 * math.pi) * running))
    return table, diagonal


def padded_rows(degree):
    rows = HALF if degree < HALF else ORDER
    base = 2 * HALF * min(degree, HALF) + 2 * ORDER * max(degree - HALF, 0)
    return rows, base


def nt_dot(left, right):
    return lax.dot_general(
        left, right, (((1,), (1,)), ((), ())), preferred_element_type=jnp.float32
    )


def kernel(
    sizes,
    diagonal,
    images,
    references,
    weight,
    weight_col,
    weight_row,
    requests,
    slot_block,
    euler,
    order,
    lane_ids,
    constants,
    coef_out,
    evidence_out,
    image_buf,
    ref_buf,
    native,
    by_angle,
    wanted,
    eulers,
    picked,
    slices,
    shares,
    dir_rows,
    cos_rows,
    sin_rows,
    table,
    averages,
    padded,
    coef,
    ang_recv,
    rot_send,
    rot_recv,
    load_sem,
    req_sem,
    eul_sem,
    slice_sem,
    share_sem,
    ang_sem,
    rot_sem,
):
    owners, shell_size, ang_size, shells, angles, rots = sizes
    half = shells * angles
    cs = 2 * shells
    slots = owners * CPO
    dirs = slots * angles
    rows_out = COEF // (owners * ang_size)
    rot = lax.axis_index("rot")
    shell = lax.axis_index("shell")
    ang = lax.axis_index("ang")
    sharers = shell_size * ang_size
    lin = shell * ang_size + ang

    load_refs = pltpu.make_async_copy(references, ref_buf, load_sem.at[0])
    load_refs.start()
    columns = order.shape[1] // LANES
    load_images = []
    for h in range(columns):
        load_images.append(
            pltpu.make_async_copy(
                images.at[:, h * LANES : (h + 1) * LANES], image_buf.at[h], load_sem.at[1 + h]
            )
        )
        load_images[-1].start()

    rot_ids = [{"rot": lax.rem(rot + k, owners)} for k in range(1, owners)]
    share_ids = []
    for k in range(1, sharers):
        other = lax.rem(lin + k, sharers)
        share_ids.append({"shell": other // ang_size, "ang": lax.rem(other, ang_size)})
    barrier = pltpu.get_barrier_semaphore()
    for device in rot_ids + share_ids:
        pl.semaphore_signal(barrier, inc=1, device_id=device, device_id_type=MESH)
    pl.semaphore_wait(barrier, len(rot_ids) + len(share_ids))

    def send(src, dst, sems, device):
        copy = pltpu.make_async_remote_copy(
            src_ref=src,
            dst_ref=dst,
            send_sem=sems[0],
            recv_sem=sems[1],
            device_id=device,
            device_id_type=MESH,
        )
        copy.start()
        return copy

    sent = []
    small = []
    for k, device in enumerate(rot_ids):
        small.append(
            send(requests.at[device["rot"]], wanted.at[rot],
                 (req_sem.at[0, k], req_sem.at[1, k]), device)
        )
        small.append(send(euler, eulers.at[rot], (eul_sem.at[0, k], eul_sem.at[1, k]), device))
    wanted[rot] = requests[rot]
    eulers[rot] = euler[...]
    for copy in small:
        copy.wait_recv()
    sent += small

    load_refs.wait()
    ids = wanted[...].reshape(slots, LANES)[:, :1]
    selector = (ids == lax.broadcasted_iota(jnp.int32, (slots, rots), 1)).astype(jnp.float32)
    selector = selector.astype(jnp.bfloat16)
    for part in range(2):
        step = min(half, 1024)
        for start in range(0, half, step):
            found = nt_dot(selector, ref_buf[part * half + start : part * half + start + step, :])
            for owner in range(owners):
                picked[owner, part, :, start : start + step] = found[
                    owner * CPO : (owner + 1) * CPO
                ]
    for owner in range(owners):
        slices[owner] = picked[owner].reshape(2 * CPO, half).astype(jnp.bfloat16)
    moving = []
    for k, device in enumerate(rot_ids):
        moving.append(
            send(
                slices.at[device["rot"]],
                slices.at[owners + rot],
                (slice_sem.at[0, k], slice_sem.at[1, k]),
                device,
            )
        )
    slices[owners + rot] = slices[rot]

    for copy in load_images:
        copy.wait()

    @pl.loop(0, shells)
    def _(s):
        scale = weight[s]
        for part in range(2):
            at = pl.ds(pl.multiple_of(part * half + s * angles, angles), angles)
            for h in range(columns):
                native[at, h * LANES : (h + 1) * LANES] = (image_buf[h, at, :] * scale).astype(
                    jnp.bfloat16
                )

    for a in range(angles):
        for h in range(columns):
            by_angle[a * cs : (a + 1) * cs, h * LANES : (h + 1) * LANES] = (
                image_buf[h, pl.ds(a, cs, stride=angles), :] * weight_col[...]
            ).astype(jnp.bfloat16)

    dev_images = order.shape[1]
    member = order[...] == lax.broadcasted_iota(jnp.int32, (dev_images, dev_images), 0)
    member = member.astype(jnp.float32).astype(jnp.bfloat16)
    blocks = dev_images // BLOCK
    place = lax.broadcasted_iota(jnp.int32, (8, dev_images), 1)
    block_of = jnp.zeros((8, dev_images), jnp.float32)
    for b in range(1, blocks):
        block_of = jnp.where(place >= b * BLOCK, float(b), block_of)
    image_block = nt_dot(block_of.astype(jnp.bfloat16), member)[:1]

    lane_slot = lane_ids[0:1, :]
    angle = lane_ids[1:2, :] + (ang * angles).astype(jnp.float32)
    rows3 = [jnp.zeros((1, dirs), jnp.float32) for _ in range(3)]
    row_slot = lax.broadcasted_iota(jnp.int32, (CPO, dirs), 0).astype(jnp.float32)
    for owner in range(owners):
        hit = requests[owner][:, :1] == lax.broadcasted_iota(jnp.int32, (CPO, rots), 1)
        here = lane_slot == row_slot + float(owner * CPO)
        for i in range(3):
            value = jnp.sum(
                jnp.where(hit, eulers[owner][i : i + 1, :], 0.0), axis=1, keepdims=True
            )
            rows3[i] += jnp.sum(jnp.where(here, value, 0.0), axis=0, keepdims=True)
    phase = (2.0 * math.pi / ANGLES) * angle + rows3[2]
    cos_p, sin_p = jnp.cos(phase), jnp.sin(phase)
    cos_a, sin_a = jnp.cos(rows3[0]), jnp.sin(rows3[0])
    cos_b, sin_b = jnp.cos(rows3[1]), jnp.sin(rows3[1])
    x = cos_a * cos_b * cos_p - sin_a * sin_p
    y = sin_a * cos_b * cos_p + cos_a * sin_p
    dir_rows[...] = -sin_b * cos_p
    real = jnp.ones_like(x)
    imag = jnp.zeros_like(x)
    for m in range(ORDER):
        factor = math.sqrt(2.0) if m else 1.0
        cos_rows[m : m + 1, :] = real * factor
        sin_rows[m : m + 1, :] = imag * factor
        real, imag = x * real - y * imag, x * imag + y * real

    width = min(CHUNK, dirs)

    @pl.loop(0, dirs // width)
    def _(step):
        lanes = pl.ds(pl.multiple_of(step * width, width), width)
        z = dir_rows[:, lanes]
        prev = jnp.zeros((HALF, width), jnp.float32)
        early = prev
        for degree in range(ORDER):
            rows, base = padded_rows(degree)
            if degree == HALF:
                pad = jnp.zeros((ORDER - HALF, width), jnp.float32)
                prev = jnp.concatenate([prev, pad], axis=0)
                early = jnp.concatenate([early, pad], axis=0)
            first = constants[:rows, degree : degree + 1]
            second = constants[:rows, ORDER + degree : ORDER + degree + 1]
            now = first * (z * prev - second * early)
            azimuth = lax.broadcasted_iota(jnp.int32, (rows, width), 0)
            now = jnp.where(azimuth == degree, diagonal[degree], now)
            table[base : base + rows, lanes] = (now * cos_rows[:rows, lanes]).astype(jnp.bfloat16)
            table[base + rows : base + 2 * rows, lanes] = (now * sin_rows[:rows, lanes]).astype(
                jnp.bfloat16
            )
            prev, early = now, prev

    for copy in moving:
        copy.wait_recv()
    sent += moving
    got = slices[owners:].reshape(owners * 2 * CPO, half)
    squares = jnp.square(got.astype(jnp.float32)) * weight_row[...]
    norms = jnp.sum(squares, axis=1, keepdims=True)
    low = jnp.dot(got, native[:half, :], preferred_element_type=jnp.float32)
    high = jnp.dot(got, native[half:, :], preferred_element_type=jnp.float32)
    low = (2.0 * low - norms).reshape(owners, 2, CPO, dev_images)[:, 0]
    high = (2.0 * high - norms).reshape(owners, 2, CPO, dev_images)[:, 1]
    shares[lin] = (low + high).reshape(slots, dev_images)
    moving = []
    for k, device in enumerate(share_ids):
        moving.append(
            send(shares.at[lin], shares.at[lin], (share_sem.at[0, k], share_sem.at[1, k]), device)
        )
    for copy in moving:
        copy.wait_recv()
    sent += moving
    scores = shares[0]
    for k in range(1, sharers):
        scores = scores + shares[k]

    valid = slot_block[:, :1] == image_block
    masked = jnp.where(valid, scores, -3.0e38)
    highest = jnp.max(masked, axis=0, keepdims=True)
    total = jnp.sum(jnp.where(valid, jnp.exp(masked - highest), 0.0), axis=0, keepdims=True)
    evidence = highest + jnp.log(total)
    evidence_out[...] = evidence
    weights = jnp.where(valid, jnp.exp(masked - evidence), 0.0).astype(jnp.bfloat16)

    if cs < averages.shape[1]:
        averages[...] = jnp.zeros(averages.shape, jnp.bfloat16)
    for a in range(angles):
        averages[a * slots : (a + 1) * slots, :cs] = nt_dot(
            weights, by_angle[a * cs : (a + 1) * cs, :]
        ).astype(jnp.bfloat16)

    tile = 256

    @pl.loop(0, ROWS // tile)
    def _(step):
        at = pl.ds(pl.multiple_of(step * tile, tile), tile)
        padded[at, :] = jnp.dot(table[at, :], averages[...], preferred_element_type=jnp.float32)

    for degree in range(ORDER):
        rows, base = padded_rows(degree)
        first = degree * degree
        coef[first : first + 1, :] = padded[base : base + 1, :]
        if degree:
            coef[pl.ds(first + 1, degree, stride=2), :] = padded[base + 1 : base + 1 + degree, :]
            coef[pl.ds(first + 2, degree, stride=2), :] = padded[
                base + rows + 1 : base + rows + 1 + degree, :
            ]

    def out_rows(rot_id, ang_id):
        return pl.ds(pl.multiple_of((rot_id * ang_size + ang_id) * rows_out, rows_out), rows_out)

    turns = [lax.rem(rot + j, owners) for j in range(1, owners + 1)]
    across = []
    for j, rot_id in enumerate(turns):
        line = []
        for k in range(1, ang_size):
            other = lax.rem(ang + k, ang_size)
            line.append(
                send(
                    coef.at[out_rows(rot_id, other)],
                    ang_recv.at[k - 1, j],
                    (ang_sem.at[0, k - 1, j], ang_sem.at[1, k - 1, j]),
                    {"ang": other},
                )
            )
        across.append(line)
    moving = []
    for j, rot_id in enumerate(turns):
        total_here = coef[out_rows(rot_id, ang), :]
        for k, copy in enumerate(across[j]):
            copy.wait_recv()
            total_here = total_here + ang_recv[k, j]
        sent += across[j]
        if j < owners - 1:
            rot_send[j] = total_here.astype(jnp.bfloat16)
            moving.append(
                send(
                    rot_send.at[j],
                    rot_recv.at[j],
                    (rot_sem.at[0, j], rot_sem.at[1, j]),
                    {"rot": rot_id},
                )
            )
    for j, copy in enumerate(moving):
        copy.wait_recv()
        total_here = total_here + rot_recv[j].astype(jnp.float32)
    sent += moving
    coef_out[...] = total_here
    for copy in sent:
        copy.wait_send()


def per_device(
    images, references, noise_weight, euler_angles, candidate_count, candidate_rotation, image_order
):
    owners = lax.axis_size("rot")
    shell_size = lax.axis_size("shell")
    ang_size = lax.axis_size("ang")
    _, shells, angles, dev_images = images.shape
    rots = references.shape[3]
    features = 2 * shells * angles
    half = shells * angles
    cs = 2 * shells
    slots = owners * CPO
    dirs = slots * angles
    sharers = shell_size * ang_size
    rows_out = COEF // (owners * ang_size)
    wide = max(cs, LANES)

    place = jnp.arange(CPO)[None, :]
    offset = jnp.zeros((owners, 1), jnp.int32)
    rotation = jnp.zeros((owners, CPO), jnp.int32)
    slot_block = jnp.full((owners, CPO), -1.0, jnp.float32)
    for b in range(candidate_count.shape[0]):
        count = candidate_count[b][:, None]
        local = place - offset
        inside = (local >= 0) & (local < count)
        match = inside[:, :, None] & (local[:, :, None] == jnp.arange(CPO))
        rotation += jnp.sum(jnp.where(match, candidate_rotation[b][:, None, :], 0), axis=2)
        slot_block = jnp.where(inside, float(b), slot_block)
        offset = offset + count
    requests = jnp.broadcast_to(rotation[:, :, None], (owners, CPO, LANES))
    slot_block = jnp.broadcast_to(slot_block.reshape(slots, 1), (slots, LANES))

    table, diagonal = legendre_constants(ORDER)
    lane = np.arange(dirs)
    lane_ids = np.stack([lane % slots, lane // slots]).astype(np.float32)
    vmem = pl.BlockSpec(memory_space=pltpu.VMEM)
    hbm = pl.BlockSpec(memory_space=pl.ANY)
    smem = pl.BlockSpec(memory_space=pltpu.SMEM)
    sizes = (owners, shell_size, ang_size, shells, angles, rots)
    f32, bf16 = jnp.float32, jnp.bfloat16
    dma = pltpu.SemaphoreType.DMA
    coefficients, evidence = pl.pallas_call(
        functools.partial(kernel, sizes, diagonal),
        out_shape=(
            jax.ShapeDtypeStruct((rows_out, wide), f32),
            jax.ShapeDtypeStruct((1, dev_images), f32),
        ),
        in_specs=[hbm, hbm, smem] + [vmem] * 8,
        out_specs=(vmem, vmem),
        scratch_shapes=[
            pltpu.VMEM((dev_images // LANES, features, LANES), f32),
            pltpu.VMEM((features, rots), bf16),
            pltpu.VMEM((features, dev_images), bf16),
            pltpu.VMEM((features, dev_images), bf16),
            pltpu.VMEM((owners, CPO, LANES), jnp.int32),
            pltpu.VMEM((owners, 3, rots), f32),
            pltpu.VMEM((owners, 2, CPO, half), f32),
            pltpu.VMEM((2 * owners, 2 * CPO, half), bf16),
            pltpu.VMEM((sharers, slots, dev_images), f32),
            pltpu.VMEM((1, dirs), f32),
            pltpu.VMEM((ORDER, dirs), f32),
            pltpu.VMEM((ORDER, dirs), f32),
            pltpu.VMEM((ROWS, dirs), bf16),
            pltpu.VMEM((dirs, wide), bf16),
            pltpu.VMEM((ROWS, wide), f32),
            pltpu.VMEM((COEF, wide), f32),
            pltpu.VMEM((max(ang_size - 1, 1), owners, rows_out, wide), f32),
            pltpu.VMEM((max(owners - 1, 1), rows_out, wide), bf16),
            pltpu.VMEM((max(owners - 1, 1), rows_out, wide), bf16),
            dma((1 + dev_images // LANES,)),
            dma((2, max(owners - 1, 1))),
            dma((2, max(owners - 1, 1))),
            dma((2, max(owners - 1, 1))),
            dma((2, max(sharers - 1, 1))),
            dma((2, max(ang_size - 1, 1), owners)),
            dma((2, max(owners - 1, 1))),
        ],
        compiler_params=pltpu.CompilerParams(
            collective_id=0, has_side_effects=True, vmem_limit_bytes=60 * 1024 * 1024
        ),
    )(
        images.reshape(features, dev_images),
        references.reshape(features, rots),
        noise_weight,
        jnp.concatenate([noise_weight, noise_weight])[:, None],
        jnp.repeat(noise_weight, angles)[None, :],
        requests,
        slot_block,
        euler_angles,
        image_order[None, :],
        jnp.asarray(lane_ids),
        jnp.asarray(table),
    )
    return (coefficients[:, :cs].reshape(rows_out, 2, shells), evidence.reshape(dev_images))


def solution(mesh):
    in_specs = (
        P(None, "shell", "ang", ("grp", "rot")),
        P(None, "shell", "ang", ("grp", "rot")),
        P(("grp", "shell")),
        P(None, ("grp", "rot")),
        P(("grp", "rot"), None),
        P(("grp", "rot"), None, None),
        P(("grp", "rot")),
    )
    out_specs = (P(("grp", "rot", "ang"), None, "shell"), P(("grp", "rot")))
    return jax.shard_map(
        per_device, mesh=mesh, in_specs=in_specs, out_specs=out_specs, check_vma=False
    )
```

```python
import functools
import math

import jax
import jax.numpy as jnp
import numpy as np
from jax import lax
from jax.experimental import pallas as pl
from jax.experimental.pallas import tpu as pltpu
from jax.sharding import PartitionSpec as P

ANGLES = 64
ORDER = 32
BLOCK = 128
CPO = 8
COEF = 1024
HALF = 16
ROWS = 2 * HALF * HALF + 2 * (ORDER - HALF) * ORDER
LANES = 128
CHUNK = 256
MESH = pl.DeviceIdType.MESH


def legendre_constants(degrees):
    table = np.zeros((degrees, 2 * degrees), np.float32)
    diagonal = []
    running = 1.0
    for degree in range(degrees):
        for azimuth in range(degree):
            table[azimuth, degree] = math.sqrt(
                (4.0 * degree * degree - 1.0) / (degree * degree - azimuth * azimuth)
            )
            lower_term = max((degree - 1.0) ** 2 - azimuth * azimuth, 0.0)
            lower_den = max(4.0 * (degree - 1.0) ** 2 - 1.0, 1.0)
            table[azimuth, degrees + degree] = math.sqrt(lower_term / lower_den)
        if degree > 0:
            running = running * (2.0 * degree - 1.0) / (2.0 * degree)
        diagonal.append(math.sqrt((2.0 * degree + 1.0) / (4.0 * math.pi) * running))
    return table, diagonal


def padded_rows(degree):
    rows = HALF if degree < HALF else ORDER
    base = 2 * HALF * min(degree, HALF) + 2 * ORDER * max(degree - HALF, 0)
    return rows, base


def nt_dot(left, right):
    return lax.dot_general(
        left, right, (((1,), (1,)), ((), ())), preferred_element_type=jnp.float32
    )


def kernel(
    sizes,
    diagonal,
    images,
    references,
    weight_in,
    count_in,
    rotation_in,
    euler_in,
    order_in,
    constants_in,
    out,
    image_buf,
    ref_buf,
    native,
    by_angle,
    weight_row,
    counts,
    rotations,
    euler,
    order,
    constants,
    weight_tile,
    requests,
    slot_block,
    wanted,
    eulers,
    slices,
    shares,
    dir_rows,
    cos_rows,
    sin_rows,
    table,
    averages,
    padded,
    coef,
    ang_recv,
    rot_own,
    rot_send,
    rot_recv,
    load_sem,
    req_sem,
    eul_sem,
    slice_sem,
    share_sem,
    ang_sem,
    rot_sem,
):
    owners, shell_size, ang_size, shells, angles, rots = sizes
    half = shells * angles
    cs = 2 * shells
    slots = owners * CPO
    dirs = slots * angles
    rows_out = COEF // (owners * ang_size)
    dev_images = order.shape[1]
    columns = dev_images // LANES
    blocks = counts.shape[0]
    rot = lax.axis_index("rot")
    shell = lax.axis_index("shell")
    ang = lax.axis_index("ang")
    sharers = shell_size * ang_size
    lin = shell * ang_size + ang

    loads = []

    def load(src, dst):
        copy = pltpu.make_async_copy(src, dst, load_sem.at[len(loads)])
        copy.start()
        loads.append(copy)

    load(count_in, counts)
    load(rotation_in, rotations)
    load(euler_in, euler)
    load(weight_in, weight_row)
    load(order_in, order)
    load(constants_in, constants)
    load(references, ref_buf)
    for h in range(columns):
        load(images.at[:, h * LANES : (h + 1) * LANES], image_buf.at[h])

    rot_ids = [{"rot": lax.rem(rot + k, owners)} for k in range(1, owners)]
    share_ids = []
    for k in range(1, sharers):
        other = lax.rem(lin + k, sharers)
        share_ids.append({"shell": other // ang_size, "ang": lax.rem(other, ang_size)})
    barrier = pltpu.get_barrier_semaphore()
    for device in rot_ids + share_ids:
        pl.semaphore_signal(barrier, inc=1, device_id=device, device_id_type=MESH)

    def send(src, dst, sems, device):
        copy = pltpu.make_async_remote_copy(
            src_ref=src,
            dst_ref=dst,
            send_sem=sems[0],
            recv_sem=sems[1],
            device_id=device,
            device_id_type=MESH,
        )
        copy.start()
        return copy

    for copy in loads[:3]:
        copy.wait()
    place = lax.broadcasted_iota(jnp.int32, (CPO, CPO), 0).astype(jnp.float32)
    entry = lax.broadcasted_iota(jnp.int32, (CPO, CPO), 1).astype(jnp.float32)
    for owner in range(owners):
        local = place
        rotation = jnp.zeros((CPO, 1), jnp.float32)
        block = jnp.full((CPO, CPO), -1.0, jnp.float32)
        for b in range(blocks):
            count = counts[b : b + 1, owner : owner + 1].astype(jnp.float32)
            listed = rotations[b][owner : owner + 1, :].astype(jnp.float32)
            inside = (local >= 0.0) & (local < count)
            rotation += jnp.sum(
                jnp.where(inside & (local == entry), listed, 0.0), axis=1, keepdims=True
            )
            block = jnp.where(inside, float(b), block)
            local = local - count
        requests[owner] = jnp.broadcast_to(rotation, (CPO, LANES)).astype(jnp.int32)
        slot_block[owner * CPO : (owner + 1) * CPO, :] = jnp.broadcast_to(
            block[:, :1], (CPO, LANES)
        )
    wanted[rot] = requests[rot]
    eulers[rot] = euler[...]

    pl.semaphore_wait(barrier, len(rot_ids) + len(share_ids))
    sent = []
    small = []
    for k, device in enumerate(rot_ids):
        small.append(
            send(requests.at[device["rot"]], wanted.at[rot],
                 (req_sem.at[0, k], req_sem.at[1, k]), device)
        )
    late = []
    for k, device in enumerate(rot_ids):
        late.append(send(euler, eulers.at[rot], (eul_sem.at[0, k], eul_sem.at[1, k]), device))

    loads[3].wait()
    diag = lax.broadcasted_iota(jnp.int32, (shells, shells), 0) == lax.broadcasted_iota(
        jnp.int32, (shells, shells), 1
    )
    weight_col = jnp.sum(jnp.where(diag, weight_row[...], 0.0), axis=1, keepdims=True)
    weight_tile[...] = jnp.broadcast_to(weight_col, (shells, LANES))
    shell_at = lax.broadcasted_iota(jnp.int32, (shells, half), 0) * angles
    lane_at = lax.broadcasted_iota(jnp.int32, (shells, half), 1)
    spread = (lane_at >= shell_at) & (lane_at < shell_at + angles)
    weight_lanes = jnp.sum(jnp.where(spread, weight_col, 0.0), axis=0, keepdims=True)

    for copy in loads[7:]:
        copy.wait()

    def weigh(s, carry):
        scale = weight_tile[pl.ds(s, 1), :]
        for part in range(2):
            at = pl.ds(pl.multiple_of(part * half + s * angles, angles), angles)
            for h in range(columns):
                native[at, h * LANES : (h + 1) * LANES] = (image_buf[h, at, :] * scale).astype(
                    jnp.bfloat16
                )
        return carry

    lax.fori_loop(0, shells, weigh, 0, unroll=4)

    for copy in small:
        copy.wait_recv()
    sent += small
    loads[6].wait()
    ids = wanted[...].reshape(slots, LANES)[:, :1]
    selector = (ids == lax.broadcasted_iota(jnp.int32, (slots, rots), 1)).astype(jnp.float32)
    selector = selector.astype(jnp.bfloat16)
    step = min(half, 1024)
    pieces = half // step
    moving = []
    for piece in range(pieces):
        start = piece * step
        low = nt_dot(selector, ref_buf[start : start + step, :])
        high = nt_dot(selector, ref_buf[half + start : half + start + step, :])
        for owner in range(owners):
            at = slice(owner * CPO, (owner + 1) * CPO)
            slices[owner, :, start : start + step] = jnp.concatenate(
                [low[at], high[at]], axis=0
            ).astype(jnp.bfloat16)
        line = []
        for k, device in enumerate(rot_ids):
            line.append(
                send(
                    slices.at[device["rot"], :, start : start + step],
                    slices.at[owners + rot, :, start : start + step],
                    (slice_sem.at[0, piece, k], slice_sem.at[1, piece, k]),
                    device,
                )
            )
        moving.append(line)
    slices[owners + rot] = slices[rot]

    for a in range(angles):
        for part in range(2):
            for h in range(columns):
                by_angle[
                    a * cs + part * shells : a * cs + (part + 1) * shells,
                    h * LANES : (h + 1) * LANES,
                ] = (
                    image_buf[h, pl.ds(part * half + a, shells, stride=angles), :]
                    * weight_tile[...]
                ).astype(jnp.bfloat16)

    loads[4].wait()
    member = order[...] == lax.broadcasted_iota(jnp.int32, (dev_images, dev_images), 0)
    member = member.astype(jnp.float32).astype(jnp.bfloat16)
    position = lax.broadcasted_iota(jnp.int32, (8, dev_images), 1)
    block_of = jnp.zeros((8, dev_images), jnp.float32)
    for b in range(1, blocks):
        block_of = jnp.where(position >= b * BLOCK, float(b), block_of)
    image_block = nt_dot(block_of.astype(jnp.bfloat16), member)[:1]

    for copy in late:
        copy.wait_recv()
    sent += late
    lane = lax.broadcasted_iota(jnp.int32, (1, dirs), 1).astype(jnp.float32)
    angle = jnp.floor((lane + 0.5) * (1.0 / slots))
    lane_slot = lane - angle * slots
    angle = angle + (ang * angles).astype(jnp.float32)
    rows3 = [jnp.zeros((1, dirs), jnp.float32) for _ in range(3)]
    row_slot = lax.broadcasted_iota(jnp.int32, (CPO, dirs), 0).astype(jnp.float32)
    for owner in range(owners):
        hit = requests[owner][:, :1] == lax.broadcasted_iota(jnp.int32, (CPO, rots), 1)
        here = lane_slot == row_slot + float(owner * CPO)
        for i in range(3):
            value = jnp.sum(
                jnp.where(hit, eulers[owner][i : i + 1, :], 0.0), axis=1, keepdims=True
            )
            rows3[i] += jnp.sum(jnp.where(here, value, 0.0), axis=0, keepdims=True)
    phase = (2.0 * math.pi / ANGLES) * angle + rows3[2]
    cos_p, sin_p = jnp.cos(phase), jnp.sin(phase)
    cos_a, sin_a = jnp.cos(rows3[0]), jnp.sin(rows3[0])
    cos_b, sin_b = jnp.cos(rows3[1]), jnp.sin(rows3[1])
    x = cos_a * cos_b * cos_p - sin_a * sin_p
    y = sin_a * cos_b * cos_p + cos_a * sin_p
    dir_rows[...] = -sin_b * cos_p
    real = jnp.ones_like(x)
    imag = jnp.zeros_like(x)
    for m in range(ORDER):
        factor = math.sqrt(2.0) if m else 1.0
        cos_rows[m : m + 1, :] = real * factor
        sin_rows[m : m + 1, :] = imag * factor
        real, imag = x * real - y * imag, x * imag + y * real

    loads[5].wait()
    width = min(CHUNK, dirs)

    @pl.loop(0, dirs // width)
    def _(turn):
        lanes = pl.ds(pl.multiple_of(turn * width, width), width)
        z = dir_rows[:, lanes]
        prev = jnp.zeros((HALF, width), jnp.float32)
        early = prev
        for degree in range(ORDER):
            rows, base = padded_rows(degree)
            if degree == HALF:
                pad = jnp.zeros((ORDER - HALF, width), jnp.float32)
                prev = jnp.concatenate([prev, pad], axis=0)
                early = jnp.concatenate([early, pad], axis=0)
            first = constants[:rows, degree : degree + 1]
            second = constants[:rows, ORDER + degree : ORDER + degree + 1]
            now = first * (z * prev - second * early)
            azimuth = lax.broadcasted_iota(jnp.int32, (rows, width), 0)
            now = jnp.where(azimuth == degree, diagonal[degree], now)
            table[base : base + rows, lanes] = (now * cos_rows[:rows, lanes]).astype(jnp.bfloat16)
            table[base + rows : base + 2 * rows, lanes] = (now * sin_rows[:rows, lanes]).astype(
                jnp.bfloat16
            )
            prev, early = now, prev

    partial = jnp.zeros((slots, dev_images), jnp.float32)
    for piece in range(pieces):
        for copy in moving[piece]:
            copy.wait_recv()
        sent += moving[piece]
        start = piece * step
        got = slices[owners:, :, start : start + step].reshape(owners * 2 * CPO, step)
        squares = jnp.square(got.astype(jnp.float32)) * weight_lanes[:, start : start + step]
        norms = jnp.sum(squares, axis=1, keepdims=True)
        low = jnp.dot(got, native[start : start + step, :], preferred_element_type=jnp.float32)
        high = jnp.dot(
            got, native[half + start : half + start + step, :], preferred_element_type=jnp.float32
        )
        low = (2.0 * low - norms).reshape(owners, 2, CPO, dev_images)[:, 0]
        high = (2.0 * high - norms).reshape(owners, 2, CPO, dev_images)[:, 1]
        partial = partial + (low + high).reshape(slots, dev_images)
    shares[lin] = partial
    moving = []
    for k, device in enumerate(share_ids):
        moving.append(
            send(shares.at[lin], shares.at[lin], (share_sem.at[0, k], share_sem.at[1, k]), device)
        )
    for copy in moving:
        copy.wait_recv()
    sent += moving
    scores = shares[0]
    for k in range(1, sharers):
        scores = scores + shares[k]

    valid = slot_block[:, :1] == image_block
    masked = jnp.where(valid, scores, -3.0e38)
    highest = jnp.max(masked, axis=0, keepdims=True)
    total = jnp.sum(jnp.where(valid, jnp.exp(masked - highest), 0.0), axis=0, keepdims=True)
    evidence = highest + jnp.log(total)
    weights = jnp.where(valid, jnp.exp(masked - evidence), 0.0).astype(jnp.bfloat16)

    if cs < averages.shape[1]:
        averages[...] = jnp.zeros(averages.shape, jnp.bfloat16)
    for a in range(angles):
        averages[a * slots : (a + 1) * slots, :cs] = nt_dot(
            weights, by_angle[a * cs : (a + 1) * cs, :]
        ).astype(jnp.bfloat16)

    def out_rows(rot_id, ang_id):
        return pl.ds(pl.multiple_of((rot_id * ang_size + ang_id) * rows_out, rows_out), rows_out)

    across = []

    def start_across(j):
        line = []
        for k in range(1, ang_size):
            other = lax.rem(ang + k, ang_size)
            line.append(
                send(
                    coef.at[out_rows(j, other)],
                    ang_recv.at[k - 1, j],
                    (ang_sem.at[0, k - 1, j], ang_sem.at[1, k - 1, j]),
                    {"ang": other},
                )
            )
        across.append(line)

    def toward(j):
        return pltpu.make_async_remote_copy(
            src_ref=rot_send.at[j],
            dst_ref=rot_recv.at[rot],
            send_sem=rot_sem.at[0, j],
            recv_sem=rot_sem.at[1, rot],
            device_id={"rot": j},
            device_id_type=MESH,
        )

    def start_along(j):
        total_here = coef[out_rows(j, ang), :]
        for k, copy in enumerate(across[j]):
            copy.wait_recv()
            total_here = total_here + ang_recv[k, j]

        @pl.when(rot == j)
        def _():
            rot_own[...] = total_here

        @pl.when(rot != j)
        def _():
            rot_send[j] = total_here.astype(jnp.bfloat16)
            toward(j).start()

    tile = 256
    done = 0
    degree = 0
    for block in range(ROWS // tile):
        at = slice(block * tile, (block + 1) * tile)
        padded[at, :] = jnp.dot(table[at, :], averages[...], preferred_element_type=jnp.float32)
        while degree < ORDER and sum(padded_rows(degree)) + padded_rows(degree)[0] <= at.stop:
            rows, base = padded_rows(degree)
            first = degree * degree
            coef[first : first + 1, :] = padded[base : base + 1, :]
            if degree:
                coef[pl.ds(first + 1, degree, stride=2), :] = padded[base + 1 : base + 1 + degree]
                coef[pl.ds(first + 2, degree, stride=2), :] = padded[
                    base + rows + 1 : base + rows + 1 + degree
                ]
            degree += 1
        while done < owners and (done + 1) * ang_size * rows_out <= degree * degree:
            start_across(done)
            done += 1
            if done > 1:
                start_along(done - 2)
    start_along(owners - 1)

    total_here = rot_own[...]
    for k in range(1, owners):
        source = lax.rem(rot + k, owners)
        pltpu.make_async_remote_copy(
            src_ref=rot_send.at[0],
            dst_ref=rot_recv.at[source],
            send_sem=rot_sem.at[0, 0],
            recv_sem=rot_sem.at[1, source],
            device_id={"rot": source},
            device_id_type=MESH,
        ).wait_recv()
        total_here = total_here + rot_recv[source].astype(jnp.float32)
    out[0 : total_here.shape[1], 0:rows_out] = jnp.transpose(total_here)
    for h in range(columns):
        row = total_here.shape[1] + h
        out[row : row + 1, 0:LANES] = evidence[:, h * LANES : (h + 1) * LANES]
    for copy in sent:
        copy.wait_send()
    for line in across:
        for copy in line:
            copy.wait_send()
    for j in range(owners):

        @pl.when(rot != j)
        def _():
            toward(j).wait_send()


def per_device(
    images, references, noise_weight, euler_angles, candidate_count, candidate_rotation, image_order
):
    owners = lax.axis_size("rot")
    shell_size = lax.axis_size("shell")
    ang_size = lax.axis_size("ang")
    _, shells, angles, dev_images = images.shape
    rots = references.shape[3]
    features = 2 * shells * angles
    half = shells * angles
    cs = 2 * shells
    slots = owners * CPO
    dirs = slots * angles
    sharers = shell_size * ang_size
    rows_out = COEF // (owners * ang_size)
    wide = max(cs, LANES)

    table, diagonal = legendre_constants(ORDER)
    vmem = pl.BlockSpec(memory_space=pltpu.VMEM)
    hbm = pl.BlockSpec(memory_space=pl.ANY)
    sizes = (owners, shell_size, ang_size, shells, angles, rots)
    f32, bf16 = jnp.float32, jnp.bfloat16
    dma = pltpu.SemaphoreType.DMA
    out_lanes = max(rows_out, LANES)
    columns = dev_images // LANES
    blocks = candidate_count.shape[0]
    others = max(owners - 1, 1)
    pieces = half // min(half, 1024)
    result = pl.pallas_call(
        functools.partial(kernel, sizes, diagonal),
        out_shape=jax.ShapeDtypeStruct((wide + 8, out_lanes), f32),
        in_specs=[hbm] * 8,
        out_specs=vmem,
        scratch_shapes=[
            pltpu.VMEM((columns, features, LANES), f32),
            pltpu.VMEM((features, rots), bf16),
            pltpu.VMEM((features, dev_images), bf16),
            pltpu.VMEM((features, dev_images), bf16),
            pltpu.VMEM((1, shells), f32),
            pltpu.VMEM((blocks, owners), jnp.int32),
            pltpu.VMEM((blocks, owners, CPO), jnp.int32),
            pltpu.VMEM((3, rots), f32),
            pltpu.VMEM((1, dev_images), jnp.int32),
            pltpu.VMEM(table.shape, f32),
            pltpu.VMEM((shells, LANES), f32),
            pltpu.VMEM((owners, CPO, LANES), jnp.int32),
            pltpu.VMEM((slots, LANES), f32),
            pltpu.VMEM((owners, CPO, LANES), jnp.int32),
            pltpu.VMEM((owners, 3, rots), f32),
            pltpu.VMEM((2 * owners, 2 * CPO, half), bf16),
            pltpu.VMEM((sharers, slots, dev_images), f32),
            pltpu.VMEM((1, dirs), f32),
            pltpu.VMEM((ORDER, dirs), f32),
            pltpu.VMEM((ORDER, dirs), f32),
            pltpu.VMEM((ROWS, dirs), bf16),
            pltpu.VMEM((dirs, wide), bf16),
            pltpu.VMEM((ROWS, wide), f32),
            pltpu.VMEM((COEF, wide), f32),
            pltpu.VMEM((max(ang_size - 1, 1), owners, rows_out, wide), f32),
            pltpu.VMEM((rows_out, wide), f32),
            pltpu.VMEM((owners, rows_out, wide), bf16),
            pltpu.VMEM((owners, rows_out, wide), bf16),
            dma((7 + columns,)),
            dma((2, others)),
            dma((2, others)),
            dma((2, pieces, others)),
            dma((2, max(sharers - 1, 1))),
            dma((2, max(ang_size - 1, 1), owners)),
            dma((2, owners)),
        ],
        compiler_params=pltpu.CompilerParams(
            collective_id=0, has_side_effects=True, vmem_limit_bytes=60 * 1024 * 1024
        ),
    )(
        images.reshape(features, dev_images),
        references.reshape(features, rots),
        noise_weight[None, :],
        candidate_count,
        candidate_rotation,
        euler_angles,
        image_order[None, :],
        jnp.asarray(table),
    )
    coefficients = jnp.transpose(result[:cs, :rows_out]).reshape(rows_out, 2, shells)
    evidence = result[wide : wide + columns, :LANES].reshape(dev_images)
    return (coefficients, evidence)


def solution(mesh):
    in_specs = (
        P(None, "shell", "ang", ("grp", "rot")),
        P(None, "shell", "ang", ("grp", "rot")),
        P(("grp", "shell")),
        P(None, ("grp", "rot")),
        P(("grp", "rot"), None),
        P(("grp", "rot"), None, None),
        P(("grp", "rot")),
    )
    out_specs = (P(("grp", "rot", "ang"), None, "shell"), P(("grp", "rot")))
    return jax.shard_map(
        per_device, mesh=mesh, in_specs=in_specs, out_specs=out_specs, check_vma=False
    )
```

```python
import functools
import math

import jax
import jax.numpy as jnp
import numpy as np
from jax import lax
from jax.experimental import pallas as pl
from jax.experimental.pallas import tpu as pltpu
from jax.sharding import PartitionSpec as P

ANGLES = 64
ORDER = 32
BLOCK = 128
CPO = 8
COEF = 1024
HALF = 16
ROWS = 2 * HALF * HALF + 2 * (ORDER - HALF) * ORDER
LANES = 128
CHUNK = 256
MESH = pl.DeviceIdType.MESH


def legendre_constants(degrees):
    table = np.zeros((degrees, 2 * degrees), np.float32)
    diagonal = []
    running = 1.0
    for degree in range(degrees):
        for azimuth in range(degree):
            table[azimuth, degree] = math.sqrt(
                (4.0 * degree * degree - 1.0) / (degree * degree - azimuth * azimuth)
            )
            lower_term = max((degree - 1.0) ** 2 - azimuth * azimuth, 0.0)
            lower_den = max(4.0 * (degree - 1.0) ** 2 - 1.0, 1.0)
            table[azimuth, degrees + degree] = math.sqrt(lower_term / lower_den)
        if degree > 0:
            running = running * (2.0 * degree - 1.0) / (2.0 * degree)
        diagonal.append(math.sqrt((2.0 * degree + 1.0) / (4.0 * math.pi) * running))
    return table, diagonal


def padded_rows(degree):
    rows = HALF if degree < HALF else ORDER
    base = 2 * HALF * min(degree, HALF) + 2 * ORDER * max(degree - HALF, 0)
    return rows, base


def nt_dot(left, right):
    return lax.dot_general(
        left, right, (((1,), (1,)), ((), ())), preferred_element_type=jnp.float32
    )


def kernel(
    sizes,
    diagonal,
    images,
    references,
    weight_in,
    count_in,
    rotation_in,
    euler_in,
    order_in,
    constants_in,
    out,
    evidence_out,
    image_buf,
    ref_buf,
    native,
    by_angle,
    weight_row,
    counts,
    rotations,
    euler,
    order,
    constants,
    weight_tile,
    requests,
    slot_block,
    wanted,
    eulers,
    slices,
    shares,
    dir_rows,
    cos_rows,
    sin_rows,
    table,
    averages,
    padded,
    coef,
    ang_recv,
    rot_own,
    rot_send,
    rot_recv,
    load_sem,
    req_sem,
    eul_sem,
    slice_sem,
    share_sem,
    ang_sem,
    rot_sem,
):
    owners, shell_size, ang_size, shells, angles, rots = sizes
    half = shells * angles
    cs = 2 * shells
    slots = owners * CPO
    dirs = slots * angles
    rows_out = COEF // (owners * ang_size)
    dev_images = order.shape[1]
    columns = dev_images // LANES
    blocks = counts.shape[0]
    rot = lax.axis_index("rot")
    shell = lax.axis_index("shell")
    ang = lax.axis_index("ang")
    sharers = shell_size * ang_size
    lin = shell * ang_size + ang

    loads = []

    def load(src, dst):
        copy = pltpu.make_async_copy(src, dst, load_sem.at[len(loads)])
        copy.start()
        loads.append(copy)

    load(count_in, counts)
    load(rotation_in, rotations)
    load(euler_in, euler)
    load(weight_in, weight_row)
    load(order_in, order)
    load(constants_in, constants)
    load(references, ref_buf)
    for h in range(columns):
        load(images.at[:, h * LANES : (h + 1) * LANES], image_buf.at[h])

    hops = sorted(range(1, owners), key=lambda k: abs(2 * k - owners))
    rot_ids = [{"rot": lax.rem(rot + k, owners)} for k in hops]
    share_ids = []
    for k in range(1, sharers):
        other = lax.rem(lin + k, sharers)
        share_ids.append({"shell": other // ang_size, "ang": lax.rem(other, ang_size)})
    barrier = pltpu.get_barrier_semaphore()
    for device in rot_ids + share_ids:
        pl.semaphore_signal(barrier, inc=1, device_id=device, device_id_type=MESH)

    def send(src, dst, sems, device):
        copy = pltpu.make_async_remote_copy(
            src_ref=src,
            dst_ref=dst,
            send_sem=sems[0],
            recv_sem=sems[1],
            device_id=device,
            device_id_type=MESH,
        )
        copy.start()
        return copy

    for copy in loads[:3]:
        copy.wait()
    place = lax.broadcasted_iota(jnp.int32, (CPO, CPO), 0).astype(jnp.float32)
    entry = lax.broadcasted_iota(jnp.int32, (CPO, CPO), 1).astype(jnp.float32)
    for owner in range(owners):
        local = place
        rotation = jnp.zeros((CPO, 1), jnp.float32)
        block = jnp.full((CPO, CPO), -1.0, jnp.float32)
        for b in range(blocks):
            count = counts[b : b + 1, owner : owner + 1].astype(jnp.float32)
            listed = rotations[b][owner : owner + 1, :].astype(jnp.float32)
            inside = (local >= 0.0) & (local < count)
            rotation += jnp.sum(
                jnp.where(inside & (local == entry), listed, 0.0), axis=1, keepdims=True
            )
            block = jnp.where(inside, float(b), block)
            local = local - count
        requests[owner] = jnp.broadcast_to(rotation, (CPO, LANES)).astype(jnp.int32)
        slot_block[owner * CPO : (owner + 1) * CPO, :] = jnp.broadcast_to(
            block[:, :1], (CPO, LANES)
        )
    wanted[rot] = requests[rot]
    eulers[rot] = euler[...]

    pl.semaphore_wait(barrier, len(rot_ids) + len(share_ids))
    sent = []
    small = []
    for k, device in enumerate(rot_ids):
        small.append(
            send(requests.at[device["rot"]], wanted.at[rot],
                 (req_sem.at[0, k], req_sem.at[1, k]), device)
        )
    late = []
    for k, device in enumerate(rot_ids):
        late.append(send(euler, eulers.at[rot], (eul_sem.at[0, k], eul_sem.at[1, k]), device))

    loads[3].wait()
    diag = lax.broadcasted_iota(jnp.int32, (shells, shells), 0) == lax.broadcasted_iota(
        jnp.int32, (shells, shells), 1
    )
    weight_col = jnp.sum(jnp.where(diag, weight_row[...], 0.0), axis=1, keepdims=True)
    weight_tile[...] = jnp.broadcast_to(weight_col, (shells, LANES))
    shell_at = lax.broadcasted_iota(jnp.int32, (shells, half), 0) * angles
    lane_at = lax.broadcasted_iota(jnp.int32, (shells, half), 1)
    spread = (lane_at >= shell_at) & (lane_at < shell_at + angles)
    weight_lanes = jnp.sum(jnp.where(spread, weight_col, 0.0), axis=0, keepdims=True)

    for copy in loads[7:]:
        copy.wait()

    def weigh(s, carry):
        scale = weight_tile[pl.ds(s, 1), :]
        for part in range(2):
            at = pl.ds(pl.multiple_of(part * half + s * angles, angles), angles)
            for h in range(columns):
                native[at, h * LANES : (h + 1) * LANES] = (image_buf[h, at, :] * scale).astype(
                    jnp.bfloat16
                )
        return carry

    lax.fori_loop(0, shells, weigh, 0, unroll=4)

    for copy in small:
        copy.wait_recv()
    sent += small
    loads[6].wait()
    ids = wanted[...].reshape(slots, LANES)[:, :1]
    selector = (ids == lax.broadcasted_iota(jnp.int32, (slots, rots), 1)).astype(jnp.float32)
    selector = selector.astype(jnp.bfloat16)
    step = min(half, 1024)
    pieces = half // step
    moving = []
    for piece in range(pieces):
        start = piece * step
        low = nt_dot(selector, ref_buf[start : start + step, :])
        high = nt_dot(selector, ref_buf[half + start : half + start + step, :])
        for owner in range(owners):
            at = slice(owner * CPO, (owner + 1) * CPO)
            slices[owner, :, start : start + step] = jnp.concatenate(
                [low[at], high[at]], axis=0
            ).astype(jnp.bfloat16)
        line = []
        for k, device in enumerate(rot_ids):
            line.append(
                send(
                    slices.at[device["rot"], :, start : start + step],
                    slices.at[owners + rot, :, start : start + step],
                    (slice_sem.at[0, piece, k], slice_sem.at[1, piece, k]),
                    device,
                )
            )
        moving.append(line)
    slices[owners + rot] = slices[rot]

    loads[4].wait()
    member = order[...] == lax.broadcasted_iota(jnp.int32, (dev_images, dev_images), 0)
    member = member.astype(jnp.float32).astype(jnp.bfloat16)
    position = lax.broadcasted_iota(jnp.int32, (8, dev_images), 1)
    block_of = jnp.zeros((8, dev_images), jnp.float32)
    for b in range(1, blocks):
        block_of = jnp.where(position >= b * BLOCK, float(b), block_of)
    image_block = nt_dot(block_of.astype(jnp.bfloat16), member)[:1]

    for copy in late:
        copy.wait_recv()
    sent += late
    lane = lax.broadcasted_iota(jnp.int32, (1, dirs), 1).astype(jnp.float32)
    angle = jnp.floor((lane + 0.5) * (1.0 / slots))
    lane_slot = lane - angle * slots
    angle = angle + (ang * angles).astype(jnp.float32)
    rows3 = [jnp.zeros((1, dirs), jnp.float32) for _ in range(3)]
    row_slot = lax.broadcasted_iota(jnp.int32, (CPO, dirs), 0).astype(jnp.float32)
    for owner in range(owners):
        hit = requests[owner][:, :1] == lax.broadcasted_iota(jnp.int32, (CPO, rots), 1)
        here = lane_slot == row_slot + float(owner * CPO)
        for i in range(3):
            value = jnp.sum(
                jnp.where(hit, eulers[owner][i : i + 1, :], 0.0), axis=1, keepdims=True
            )
            rows3[i] += jnp.sum(jnp.where(here, value, 0.0), axis=0, keepdims=True)
    phase = (2.0 * math.pi / ANGLES) * angle + rows3[2]
    stacked = jnp.concatenate([rows3[0], rows3[1], phase], axis=0)
    cosines, sines = jnp.cos(stacked), jnp.sin(stacked)
    cos_a, cos_b, cos_p = cosines[0:1], cosines[1:2], cosines[2:3]
    sin_a, sin_b, sin_p = sines[0:1], sines[1:2], sines[2:3]
    x = cos_a * cos_b * cos_p - sin_a * sin_p
    y = sin_a * cos_b * cos_p + cos_a * sin_p
    dir_rows[...] = -sin_b * cos_p
    real = jnp.ones_like(x)
    imag = jnp.zeros_like(x)
    for m in range(ORDER):
        factor = math.sqrt(2.0) if m else 1.0
        cos_rows[m : m + 1, :] = real * factor
        sin_rows[m : m + 1, :] = imag * factor
        real, imag = x * real - y * imag, x * imag + y * real

    loads[5].wait()
    width = min(CHUNK, dirs)

    @pl.loop(0, dirs // width)
    def _(turn):
        lanes = pl.ds(pl.multiple_of(turn * width, width), width)
        z = dir_rows[:, lanes]
        prev = jnp.zeros((HALF, width), jnp.float32)
        early = prev
        for degree in range(ORDER):
            rows, base = padded_rows(degree)
            if degree == HALF:
                pad = jnp.zeros((ORDER - HALF, width), jnp.float32)
                prev = jnp.concatenate([prev, pad], axis=0)
                early = jnp.concatenate([early, pad], axis=0)
            first = constants[:rows, degree : degree + 1]
            second = constants[:rows, ORDER + degree : ORDER + degree + 1]
            now = first * (z * prev - second * early)
            azimuth = lax.broadcasted_iota(jnp.int32, (rows, width), 0)
            now = jnp.where(azimuth == degree, diagonal[degree], now)
            table[base : base + rows, lanes] = (now * cos_rows[:rows, lanes]).astype(jnp.bfloat16)
            table[base + rows : base + 2 * rows, lanes] = (now * sin_rows[:rows, lanes]).astype(
                jnp.bfloat16
            )
            prev, early = now, prev

    partial = jnp.zeros((slots, dev_images), jnp.float32)
    for piece in range(pieces):
        for copy in moving[piece]:
            copy.wait_recv()
        sent += moving[piece]
        start = piece * step
        got = slices[owners:, :, start : start + step].reshape(owners * 2 * CPO, step)
        squares = jnp.square(got.astype(jnp.float32)) * weight_lanes[:, start : start + step]
        norms = jnp.sum(squares, axis=1, keepdims=True)
        low = jnp.dot(got, native[start : start + step, :], preferred_element_type=jnp.float32)
        high = jnp.dot(
            got, native[half + start : half + start + step, :], preferred_element_type=jnp.float32
        )
        low = (2.0 * low - norms).reshape(owners, 2, CPO, dev_images)[:, 0]
        high = (2.0 * high - norms).reshape(owners, 2, CPO, dev_images)[:, 1]
        partial = partial + (low + high).reshape(slots, dev_images)
    shares[lin] = partial
    moving = []
    for k, device in enumerate(share_ids):
        moving.append(
            send(shares.at[lin], shares.at[lin], (share_sem.at[0, k], share_sem.at[1, k]), device)
        )
    for a in range(angles):
        for part in range(2):
            for h in range(columns):
                by_angle[
                    a * cs + part * shells : a * cs + (part + 1) * shells,
                    h * LANES : (h + 1) * LANES,
                ] = (
                    image_buf[h, pl.ds(part * half + a, shells, stride=angles), :]
                    * weight_tile[...]
                ).astype(jnp.bfloat16)

    for copy in moving:
        copy.wait_recv()
    sent += moving
    scores = shares[0]
    for k in range(1, sharers):
        scores = scores + shares[k]

    valid = slot_block[:, :1] == image_block
    masked = jnp.where(valid, scores, -3.0e38)
    highest = jnp.max(masked, axis=0, keepdims=True)
    total = jnp.sum(jnp.where(valid, jnp.exp(masked - highest), 0.0), axis=0, keepdims=True)
    evidence = highest + jnp.log(total)
    evidence_out[...] = evidence
    weights = jnp.where(valid, jnp.exp(masked - evidence), 0.0).astype(jnp.bfloat16)

    if cs < averages.shape[1]:
        averages[...] = jnp.zeros(averages.shape, jnp.bfloat16)
    per = 2 if cs % LANES == 0 and angles % 2 == 0 else 1
    for a in range(0, angles, per):
        pair = nt_dot(weights, by_angle[a * cs : (a + per) * cs, :]).astype(jnp.bfloat16)
        for i in range(per):
            averages[(a + i) * slots : (a + i + 1) * slots, :cs] = pair[:, i * cs : (i + 1) * cs]

    def out_rows(rot_id, ang_id):
        return pl.ds(pl.multiple_of((rot_id * ang_size + ang_id) * rows_out, rows_out), rows_out)

    across = []

    def start_across(j):
        line = []
        for k in range(1, ang_size):
            other = lax.rem(ang + k, ang_size)
            line.append(
                send(
                    coef.at[out_rows(j, other)],
                    ang_recv.at[k - 1, j],
                    (ang_sem.at[0, k - 1, j], ang_sem.at[1, k - 1, j]),
                    {"ang": other},
                )
            )
        across.append(line)

    def toward(j):
        return pltpu.make_async_remote_copy(
            src_ref=rot_send.at[j],
            dst_ref=rot_recv.at[rot],
            send_sem=rot_sem.at[0, j],
            recv_sem=rot_sem.at[1, rot],
            device_id={"rot": j},
            device_id_type=MESH,
        )

    def start_along(j):
        total_here = coef[out_rows(j, ang), :]
        for k, copy in enumerate(across[j]):
            copy.wait_recv()
            total_here = total_here + ang_recv[k, j]

        @pl.when(rot == j)
        def _():
            rot_own[...] = total_here

        @pl.when(rot != j)
        def _():
            rot_send[j] = total_here.astype(jnp.bfloat16)
            toward(j).start()

    tile = 256
    done = 0
    degree = 0
    for block in range(ROWS // tile):
        at = slice(block * tile, (block + 1) * tile)
        padded[at, :] = jnp.dot(table[at, :], averages[...], preferred_element_type=jnp.float32)
        while degree < ORDER and sum(padded_rows(degree)) + padded_rows(degree)[0] <= at.stop:
            rows, base = padded_rows(degree)
            first = degree * degree
            coef[first : first + 1, :] = padded[base : base + 1, :]
            if degree:
                coef[pl.ds(first + 1, degree, stride=2), :] = padded[base + 1 : base + 1 + degree]
                coef[pl.ds(first + 2, degree, stride=2), :] = padded[
                    base + rows + 1 : base + rows + 1 + degree
                ]
            degree += 1
        while done < owners and (done + 1) * ang_size * rows_out <= degree * degree:
            start_across(done)
            done += 1
            if done > 1:
                start_along(done - 2)
    start_along(owners - 1)

    total_here = rot_own[...]
    for k in range(1, owners):
        source = lax.rem(rot + k, owners)
        pltpu.make_async_remote_copy(
            src_ref=rot_send.at[0],
            dst_ref=rot_recv.at[source],
            send_sem=rot_sem.at[0, 0],
            recv_sem=rot_sem.at[1, source],
            device_id={"rot": source},
            device_id_type=MESH,
        ).wait_recv()
        total_here = total_here + rot_recv[source].astype(jnp.float32)
    out[...] = jnp.transpose(total_here)[:cs]
    for copy in sent:
        copy.wait_send()
    for line in across:
        for copy in line:
            copy.wait_send()
    for j in range(owners):

        @pl.when(rot != j)
        def _():
            toward(j).wait_send()


def hand_over(coef_in, evidence_in, coef_out, evidence_out, sems):
    first = pltpu.make_async_copy(coef_in, coef_out, sems.at[0])
    second = pltpu.make_async_copy(evidence_in, evidence_out, sems.at[1])
    first.start()
    second.start()
    first.wait()
    second.wait()


def per_device(
    images, references, noise_weight, euler_angles, candidate_count, candidate_rotation, image_order
):
    owners = lax.axis_size("rot")
    shell_size = lax.axis_size("shell")
    ang_size = lax.axis_size("ang")
    _, shells, angles, dev_images = images.shape
    rots = references.shape[3]
    features = 2 * shells * angles
    half = shells * angles
    cs = 2 * shells
    slots = owners * CPO
    dirs = slots * angles
    sharers = shell_size * ang_size
    rows_out = COEF // (owners * ang_size)
    wide = max(cs, LANES)

    table, diagonal = legendre_constants(ORDER)
    vmem = pl.BlockSpec(memory_space=pltpu.VMEM)
    hbm = pl.BlockSpec(memory_space=pl.ANY)
    sizes = (owners, shell_size, ang_size, shells, angles, rots)
    f32, bf16 = jnp.float32, jnp.bfloat16
    dma = pltpu.SemaphoreType.DMA
    columns = dev_images // LANES
    blocks = candidate_count.shape[0]
    others = max(owners - 1, 1)
    pieces = half // min(half, 1024)
    coefficients, evidence = pl.pallas_call(
        functools.partial(kernel, sizes, diagonal),
        out_shape=(
            jax.ShapeDtypeStruct((cs, rows_out), f32),
            jax.ShapeDtypeStruct((1, dev_images), f32),
        ),
        in_specs=[hbm] * 8,
        out_specs=(vmem, vmem),
        scratch_shapes=[
            pltpu.VMEM((columns, features, LANES), f32),
            pltpu.VMEM((features, rots), bf16),
            pltpu.VMEM((features, dev_images), bf16),
            pltpu.VMEM((features, dev_images), bf16),
            pltpu.VMEM((1, shells), f32),
            pltpu.VMEM((blocks, owners), jnp.int32),
            pltpu.VMEM((blocks, owners, CPO), jnp.int32),
            pltpu.VMEM((3, rots), f32),
            pltpu.VMEM((1, dev_images), jnp.int32),
            pltpu.VMEM(table.shape, f32),
            pltpu.VMEM((shells, LANES), f32),
            pltpu.VMEM((owners, CPO, LANES), jnp.int32),
            pltpu.VMEM((slots, LANES), f32),
            pltpu.VMEM((owners, CPO, LANES), jnp.int32),
            pltpu.VMEM((owners, 3, rots), f32),
            pltpu.VMEM((2 * owners, 2 * CPO, half), bf16),
            pltpu.VMEM((sharers, slots, dev_images), f32),
            pltpu.VMEM((1, dirs), f32),
            pltpu.VMEM((ORDER, dirs), f32),
            pltpu.VMEM((ORDER, dirs), f32),
            pltpu.VMEM((ROWS, dirs), bf16),
            pltpu.VMEM((dirs, wide), bf16),
            pltpu.VMEM((ROWS, wide), f32),
            pltpu.VMEM((COEF, wide), f32),
            pltpu.VMEM((max(ang_size - 1, 1), owners, rows_out, wide), f32),
            pltpu.VMEM((rows_out, wide), f32),
            pltpu.VMEM((owners, rows_out, wide), bf16),
            pltpu.VMEM((owners, rows_out, wide), bf16),
            dma((7 + columns,)),
            dma((2, others)),
            dma((2, others)),
            dma((2, pieces, others)),
            dma((2, max(sharers - 1, 1))),
            dma((2, max(ang_size - 1, 1), owners)),
            dma((2, owners)),
        ],
        compiler_params=pltpu.CompilerParams(
            collective_id=0, has_side_effects=True, vmem_limit_bytes=60 * 1024 * 1024
        ),
    )(
        images.reshape(features, dev_images),
        references.reshape(features, rots),
        noise_weight[None, :],
        candidate_count,
        candidate_rotation,
        euler_angles,
        image_order[None, :],
        jnp.asarray(table),
    )
    coefficients, evidence = pl.pallas_call(
        hand_over,
        out_shape=(
            jax.ShapeDtypeStruct(coefficients.shape, f32),
            jax.ShapeDtypeStruct(evidence.shape, f32),
        ),
        in_specs=[hbm, hbm],
        out_specs=(hbm, hbm),
        scratch_shapes=[dma((2,))],
        compiler_params=pltpu.CompilerParams(vmem_limit_bytes=60 * 1024 * 1024),
    )(coefficients, evidence)
    coefficients = jnp.transpose(coefficients).reshape(rows_out, 2, shells)
    return (coefficients, evidence.reshape(dev_images))


def solution(mesh):
    in_specs = (
        P(None, "shell", "ang", ("grp", "rot")),
        P(None, "shell", "ang", ("grp", "rot")),
        P(("grp", "shell")),
        P(None, ("grp", "rot")),
        P(("grp", "rot"), None),
        P(("grp", "rot"), None, None),
        P(("grp", "rot")),
    )
    out_specs = (P(("grp", "rot", "ang"), None, "shell"), P(("grp", "rot")))
    return jax.shard_map(
        per_device, mesh=mesh, in_specs=in_specs, out_specs=out_specs, check_vma=False
    )
```

```python
import functools
import math

import jax
import jax.numpy as jnp
import numpy as np
from jax import lax
from jax.experimental import pallas as pl
from jax.experimental.pallas import tpu as pltpu
from jax.sharding import PartitionSpec as P

ANGLES = 64
ORDER = 32
BLOCK = 128
CPO = 8
COEF = 1024
HALF = 16
LANES = 128
CHUNK = 256
MESH = pl.DeviceIdType.MESH


def legendre_constants(degrees):
    table = np.zeros((degrees, 2 * degrees), np.float32)
    diagonal = []
    running = 1.0
    for degree in range(degrees):
        for azimuth in range(degree):
            table[azimuth, degree] = math.sqrt(
                (4.0 * degree * degree - 1.0) / (degree * degree - azimuth * azimuth)
            )
            lower_term = max((degree - 1.0) ** 2 - azimuth * azimuth, 0.0)
            lower_den = max(4.0 * (degree - 1.0) ** 2 - 1.0, 1.0)
            table[azimuth, degrees + degree] = math.sqrt(lower_term / lower_den)
        if degree > 0:
            running = running * (2.0 * degree - 1.0) / (2.0 * degree)
        diagonal.append(math.sqrt((2.0 * degree + 1.0) / (4.0 * math.pi) * running))
    return table, diagonal


def nt_dot(left, right):
    return lax.dot_general(
        left, right, (((1,), (1,)), ((), ())), preferred_element_type=jnp.float32
    )


def kernel(
    sizes,
    diagonal,
    images,
    references,
    weight_in,
    count_in,
    rotation_in,
    euler_in,
    order_in,
    constants_in,
    out,
    evidence_out,
    image_buf,
    ref_buf,
    native,
    by_angle,
    weight_row,
    counts,
    rotations,
    euler,
    order,
    constants,
    weight_tile,
    requests,
    slot_block,
    wanted,
    eulers,
    slices,
    shares,
    dir_rows,
    cos_rows,
    sin_rows,
    table,
    averages,
    ordered,
    coef,
    ang_recv,
    rot_send,
    rot_recv,
    load_sem,
    req_sem,
    eul_sem,
    slice_sem,
    share_sem,
    ang_sem,
    rot_sem,
):
    owners, shell_size, ang_size, shells, angles, rots = sizes
    half = shells * angles
    cs = 2 * shells
    slots = owners * CPO
    dirs = slots * angles
    rows_out = COEF // (owners * ang_size)
    dev_images = order.shape[1]
    columns = dev_images // LANES
    blocks = counts.shape[0]
    rot = lax.axis_index("rot")
    shell = lax.axis_index("shell")
    ang = lax.axis_index("ang")
    sharers = shell_size * ang_size
    lin = shell * ang_size + ang

    loads = []

    def load(src, dst):
        copy = pltpu.make_async_copy(src, dst, load_sem.at[len(loads)])
        copy.start()
        loads.append(copy)

    load(count_in, counts)
    load(rotation_in, rotations)
    load(euler_in, euler)
    load(weight_in, weight_row)
    load(order_in, order)
    load(constants_in, constants)
    load(references, ref_buf)
    for h in range(columns):
        load(images.at[:, h * LANES : (h + 1) * LANES], image_buf.at[h])

    hops = sorted(range(1, owners), key=lambda k: abs(2 * k - owners))
    rot_ids = [{"rot": lax.rem(rot + k, owners)} for k in hops]
    share_ids = []
    for k in range(1, sharers):
        other = lax.rem(lin + k, sharers)
        share_ids.append({"shell": other // ang_size, "ang": lax.rem(other, ang_size)})
    barrier = pltpu.get_barrier_semaphore()
    for device in rot_ids + share_ids:
        pl.semaphore_signal(barrier, inc=1, device_id=device, device_id_type=MESH)

    def send(src, dst, sems, device):
        copy = pltpu.make_async_remote_copy(
            src_ref=src,
            dst_ref=dst,
            send_sem=sems[0],
            recv_sem=sems[1],
            device_id=device,
            device_id_type=MESH,
        )
        copy.start()
        return copy

    for copy in loads[:3]:
        copy.wait()
    place = lax.broadcasted_iota(jnp.int32, (CPO, CPO), 0).astype(jnp.float32)
    entry = lax.broadcasted_iota(jnp.int32, (CPO, CPO), 1).astype(jnp.float32)
    for owner in range(owners):
        local = place
        rotation = jnp.zeros((CPO, 1), jnp.float32)
        block = jnp.full((CPO, CPO), -1.0, jnp.float32)
        for b in range(blocks):
            count = counts[b : b + 1, owner : owner + 1].astype(jnp.float32)
            listed = rotations[b][owner : owner + 1, :].astype(jnp.float32)
            inside = (local >= 0.0) & (local < count)
            rotation += jnp.sum(
                jnp.where(inside & (local == entry), listed, 0.0), axis=1, keepdims=True
            )
            block = jnp.where(inside, float(b), block)
            local = local - count
        requests[owner] = jnp.broadcast_to(rotation, (CPO, LANES)).astype(jnp.int32)
        slot_block[owner * CPO : (owner + 1) * CPO, :] = jnp.broadcast_to(
            block[:, :1], (CPO, LANES)
        )
    wanted[rot] = requests[rot]
    eulers[rot] = euler[...]

    pl.semaphore_wait(barrier, len(rot_ids) + len(share_ids))
    sent = []
    small = []
    for k, device in enumerate(rot_ids):
        small.append(
            send(requests.at[device["rot"]], wanted.at[rot],
                 (req_sem.at[0, k], req_sem.at[1, k]), device)
        )
    late = []
    for k, device in enumerate(rot_ids):
        late.append(send(euler, eulers.at[rot], (eul_sem.at[0, k], eul_sem.at[1, k]), device))

    loads[3].wait()
    diag = lax.broadcasted_iota(jnp.int32, (shells, shells), 0) == lax.broadcasted_iota(
        jnp.int32, (shells, shells), 1
    )
    weight_col = jnp.sum(jnp.where(diag, weight_row[...], 0.0), axis=1, keepdims=True)
    weight_tile[...] = jnp.broadcast_to(weight_col, (shells, LANES))
    shell_at = lax.broadcasted_iota(jnp.int32, (shells, half), 0) * angles
    lane_at = lax.broadcasted_iota(jnp.int32, (shells, half), 1)
    spread = (lane_at >= shell_at) & (lane_at < shell_at + angles)
    weight_lanes = jnp.sum(jnp.where(spread, weight_col, 0.0), axis=0, keepdims=True)

    for copy in loads[7:]:
        copy.wait()

    def weigh(s, carry):
        scale = weight_tile[pl.ds(s, 1), :]
        for part in range(2):
            at = pl.ds(pl.multiple_of(part * half + s * angles, angles), angles)
            for h in range(columns):
                native[at, h * LANES : (h + 1) * LANES] = (image_buf[h, at, :] * scale).astype(
                    jnp.bfloat16
                )
        return carry

    step = min(half, 1024)
    pieces = half // step
    early_shells = step // angles
    lax.fori_loop(0, early_shells, weigh, 0, unroll=4)

    for copy in small:
        copy.wait_recv()
    sent += small
    loads[6].wait()
    ids = wanted[...].reshape(slots, LANES)[:, :1]
    selector = (ids == lax.broadcasted_iota(jnp.int32, (slots, rots), 1)).astype(jnp.float32)
    selector = selector.astype(jnp.bfloat16)
    moving = []
    for piece in range(pieces):
        start = piece * step
        low = nt_dot(selector, ref_buf[start : start + step, :])
        high = nt_dot(selector, ref_buf[half + start : half + start + step, :])
        for owner in range(owners):
            at = slice(owner * CPO, (owner + 1) * CPO)
            slices[owner, :, start : start + step] = jnp.concatenate(
                [low[at], high[at]], axis=0
            ).astype(jnp.bfloat16)
        line = []
        for k, device in enumerate(rot_ids):
            line.append(
                send(
                    slices.at[device["rot"], :, start : start + step],
                    slices.at[owners + rot, :, start : start + step],
                    (slice_sem.at[0, piece, k], slice_sem.at[1, piece, k]),
                    device,
                )
            )
        moving.append(line)
    slices[owners + rot] = slices[rot]
    lax.fori_loop(early_shells, shells, weigh, 0, unroll=4)

    loads[4].wait()
    member = order[...] == lax.broadcasted_iota(jnp.int32, (dev_images, dev_images), 0)
    member = member.astype(jnp.float32).astype(jnp.bfloat16)
    position = lax.broadcasted_iota(jnp.int32, (8, dev_images), 1)
    block_of = jnp.zeros((8, dev_images), jnp.float32)
    for b in range(1, blocks):
        block_of = jnp.where(position >= b * BLOCK, float(b), block_of)
    image_block = nt_dot(block_of.astype(jnp.bfloat16), member)[:1]

    for copy in late:
        copy.wait_recv()
    sent += late
    lane = lax.broadcasted_iota(jnp.int32, (1, dirs), 1).astype(jnp.float32)
    angle = jnp.floor((lane + 0.5) * (1.0 / slots))
    lane_slot = lane - angle * slots
    angle = angle + (ang * angles).astype(jnp.float32)
    rows3 = [jnp.zeros((1, dirs), jnp.float32) for _ in range(3)]
    row_slot = lax.broadcasted_iota(jnp.int32, (CPO, dirs), 0).astype(jnp.float32)
    for owner in range(owners):
        hit = requests[owner][:, :1] == lax.broadcasted_iota(jnp.int32, (CPO, rots), 1)
        here = lane_slot == row_slot + float(owner * CPO)
        for i in range(3):
            value = jnp.sum(
                jnp.where(hit, eulers[owner][i : i + 1, :], 0.0), axis=1, keepdims=True
            )
            rows3[i] += jnp.sum(jnp.where(here, value, 0.0), axis=0, keepdims=True)
    phase = (2.0 * math.pi / ANGLES) * angle + rows3[2]
    stacked = jnp.concatenate([rows3[0], rows3[1], phase], axis=0)
    cosines, sines = jnp.cos(stacked), jnp.sin(stacked)
    cos_a, cos_b, cos_p = cosines[0:1], cosines[1:2], cosines[2:3]
    sin_a, sin_b, sin_p = sines[0:1], sines[1:2], sines[2:3]
    x = cos_a * cos_b * cos_p - sin_a * sin_p
    y = sin_a * cos_b * cos_p + cos_a * sin_p
    dir_rows[...] = -sin_b * cos_p
    real = jnp.ones_like(x)
    imag = jnp.zeros_like(x)
    for m in range(ORDER):
        factor = math.sqrt(2.0) if m else 1.0
        cos_rows[m : m + 1, :] = real * factor
        sin_rows[m : m + 1, :] = imag * factor if m else real
        real, imag = x * real - y * imag, x * imag + y * real

    loads[5].wait()
    width = min(CHUNK, dirs)

    @pl.loop(0, dirs // width)
    def _(turn):
        lanes = pl.ds(pl.multiple_of(turn * width, width), width)
        z = dir_rows[:, lanes]
        prev = jnp.zeros((HALF, width), jnp.float32)
        early = prev
        for degree in range(ORDER):
            rows = HALF if degree < HALF else ORDER
            if degree == HALF:
                pad = jnp.zeros((ORDER - HALF, width), jnp.float32)
                prev = jnp.concatenate([prev, pad], axis=0)
                early = jnp.concatenate([early, pad], axis=0)
            first = constants[:rows, degree : degree + 1]
            second = constants[:rows, ORDER + degree : ORDER + degree + 1]
            now = first * (z * prev - second * early)
            azimuth = lax.broadcasted_iota(jnp.int32, (rows, width), 0)
            now = jnp.where(azimuth == degree, diagonal[degree], now)
            cosine = now * cos_rows[:rows, lanes]
            sine = now * sin_rows[:rows, lanes]
            first_row = degree * degree
            for h in range(width // LANES):
                at = slice(h * LANES, (h + 1) * LANES)
                ordered[h, pl.ds(first_row, degree + 1, stride=2), :] = sine[: degree + 1, at]
                if degree:
                    ordered[h, pl.ds(first_row + 1, degree, stride=2), :] = cosine[
                        1 : degree + 1, at
                    ]
            prev, early = now, prev
        for h in range(width // LANES):
            at = pl.ds(pl.multiple_of(turn * width + h * LANES, LANES), LANES)
            table[:, at] = ordered[h].astype(jnp.bfloat16)

    partial = jnp.zeros((slots, dev_images), jnp.float32)
    for piece in range(pieces):
        for copy in moving[piece]:
            copy.wait_recv()
        sent += moving[piece]
        start = piece * step
        got = slices[owners:, :, start : start + step].reshape(owners * 2 * CPO, step)
        squares = jnp.square(got.astype(jnp.float32)) * weight_lanes[:, start : start + step]
        norms = jnp.sum(squares, axis=1, keepdims=True)
        low = jnp.dot(got, native[start : start + step, :], preferred_element_type=jnp.float32)
        high = jnp.dot(
            got, native[half + start : half + start + step, :], preferred_element_type=jnp.float32
        )
        low = (2.0 * low - norms).reshape(owners, 2, CPO, dev_images)[:, 0]
        high = (2.0 * high - norms).reshape(owners, 2, CPO, dev_images)[:, 1]
        partial = partial + (low + high).reshape(slots, dev_images)
    shares[lin] = partial
    moving = []
    for k, device in enumerate(share_ids):
        moving.append(
            send(shares.at[lin], shares.at[lin], (share_sem.at[0, k], share_sem.at[1, k]), device)
        )
    for a in range(angles):
        for part in range(2):
            for h in range(columns):
                by_angle[
                    a * cs + part * shells : a * cs + (part + 1) * shells,
                    h * LANES : (h + 1) * LANES,
                ] = (
                    image_buf[h, pl.ds(part * half + a, shells, stride=angles), :]
                    * weight_tile[...]
                ).astype(jnp.bfloat16)

    for copy in moving:
        copy.wait_recv()
    sent += moving
    scores = shares[0]
    for k in range(1, sharers):
        scores = scores + shares[k]

    valid = slot_block[:, :1] == image_block
    masked = jnp.where(valid, scores, -3.0e38)
    highest = jnp.max(masked, axis=0, keepdims=True)
    total = jnp.sum(jnp.where(valid, jnp.exp(masked - highest), 0.0), axis=0, keepdims=True)
    evidence = highest + jnp.log(total)
    evidence_out[...] = evidence
    weights = jnp.where(valid, jnp.exp(masked - evidence), 0.0).astype(jnp.bfloat16)

    if cs < averages.shape[1]:
        averages[...] = jnp.zeros(averages.shape, jnp.bfloat16)
    per = 2 if cs % LANES == 0 and angles % 2 == 0 else 1
    for a in range(0, angles, per):
        pair = nt_dot(weights, by_angle[a * cs : (a + per) * cs, :]).astype(jnp.bfloat16)
        for i in range(per):
            averages[(a + i) * slots : (a + i + 1) * slots, :cs] = pair[:, i * cs : (i + 1) * cs]

    moving = []
    across = []
    turns = hops + [0]

    def start_along(i):
        total_here = coef[i, ang]
        for k, copy in enumerate(across[i]):
            copy.wait_recv()
            total_here = total_here + ang_recv[k, i]
        if i < owners - 1:
            rot_send[i] = total_here.astype(jnp.bfloat16)
            moving.append(
                send(
                    rot_send.at[i],
                    rot_recv.at[i],
                    (rot_sem.at[0, i], rot_sem.at[1, i]),
                    rot_ids[i],
                )
            )
        return total_here

    group = ang_size * rows_out
    for i, hop in enumerate(turns):
        start = pl.multiple_of(lax.rem(rot + hop, owners) * group, group)
        rows = jnp.dot(
            table[pl.ds(start, group), :], averages[...], preferred_element_type=jnp.float32
        )
        for k in range(ang_size):
            coef[i, k] = rows[k * rows_out : (k + 1) * rows_out]
        line = []
        for k in range(1, ang_size):
            other = lax.rem(ang + k, ang_size)
            line.append(
                send(
                    coef.at[i, other],
                    ang_recv.at[k - 1, i],
                    (ang_sem.at[0, k - 1, i], ang_sem.at[1, k - 1, i]),
                    {"ang": other},
                )
            )
        across.append(line)
        if i:
            start_along(i - 1)
    total_here = start_along(owners - 1)
    for i, copy in enumerate(moving):
        copy.wait_recv()
        total_here = total_here + rot_recv[i].astype(jnp.float32)
    sent += moving
    out[...] = jnp.transpose(total_here)[:cs]
    for copy in sent:
        copy.wait_send()
    for line in across:
        for copy in line:
            copy.wait_send()


def hand_over(coef_in, evidence_in, coef_out, evidence_out):
    coef_out[...] = coef_in[...]
    evidence_out[...] = evidence_in[...]


def per_device(
    images, references, noise_weight, euler_angles, candidate_count, candidate_rotation, image_order
):
    owners = lax.axis_size("rot")
    shell_size = lax.axis_size("shell")
    ang_size = lax.axis_size("ang")
    _, shells, angles, dev_images = images.shape
    rots = references.shape[3]
    features = 2 * shells * angles
    half = shells * angles
    cs = 2 * shells
    slots = owners * CPO
    dirs = slots * angles
    sharers = shell_size * ang_size
    rows_out = COEF // (owners * ang_size)
    wide = max(cs, LANES)

    table, diagonal = legendre_constants(ORDER)
    vmem = pl.BlockSpec(memory_space=pltpu.VMEM)
    hbm = pl.BlockSpec(memory_space=pl.ANY)
    sizes = (owners, shell_size, ang_size, shells, angles, rots)
    f32, bf16 = jnp.float32, jnp.bfloat16
    dma = pltpu.SemaphoreType.DMA
    columns = dev_images // LANES
    blocks = candidate_count.shape[0]
    others = max(owners - 1, 1)
    pieces = half // min(half, 1024)
    coefficients, evidence = pl.pallas_call(
        functools.partial(kernel, sizes, diagonal),
        out_shape=(
            jax.ShapeDtypeStruct((cs, rows_out), f32),
            jax.ShapeDtypeStruct((1, dev_images), f32),
        ),
        in_specs=[hbm] * 8,
        out_specs=(vmem, vmem),
        scratch_shapes=[
            pltpu.VMEM((columns, features, LANES), f32),
            pltpu.VMEM((features, rots), bf16),
            pltpu.VMEM((features, dev_images), bf16),
            pltpu.VMEM((features, dev_images), bf16),
            pltpu.VMEM((1, shells), f32),
            pltpu.VMEM((blocks, owners), jnp.int32),
            pltpu.VMEM((blocks, owners, CPO), jnp.int32),
            pltpu.VMEM((3, rots), f32),
            pltpu.VMEM((1, dev_images), jnp.int32),
            pltpu.VMEM(table.shape, f32),
            pltpu.VMEM((shells, LANES), f32),
            pltpu.VMEM((owners, CPO, LANES), jnp.int32),
            pltpu.VMEM((slots, LANES), f32),
            pltpu.VMEM((owners, CPO, LANES), jnp.int32),
            pltpu.VMEM((owners, 3, rots), f32),
            pltpu.VMEM((2 * owners, 2 * CPO, half), bf16),
            pltpu.VMEM((sharers, slots, dev_images), f32),
            pltpu.VMEM((1, dirs), f32),
            pltpu.VMEM((ORDER, dirs), f32),
            pltpu.VMEM((ORDER, dirs), f32),
            pltpu.VMEM((COEF, dirs), bf16),
            pltpu.VMEM((dirs, wide), bf16),
            pltpu.VMEM((min(CHUNK, dirs) // LANES, COEF, LANES), f32),
            pltpu.VMEM((owners, ang_size, rows_out, wide), f32),
            pltpu.VMEM((max(ang_size - 1, 1), owners, rows_out, wide), f32),
            pltpu.VMEM((others, rows_out, wide), bf16),
            pltpu.VMEM((others, rows_out, wide), bf16),
            dma((7 + columns,)),
            dma((2, others)),
            dma((2, others)),
            dma((2, pieces, others)),
            dma((2, max(sharers - 1, 1))),
            dma((2, max(ang_size - 1, 1), owners)),
            dma((2, others)),
        ],
        compiler_params=pltpu.CompilerParams(
            collective_id=0, has_side_effects=True, vmem_limit_bytes=60 * 1024 * 1024
        ),
    )(
        images.reshape(features, dev_images),
        references.reshape(features, rots),
        noise_weight[None, :],
        candidate_count,
        candidate_rotation,
        euler_angles,
        image_order[None, :],
        jnp.asarray(table),
    )
    coefficients, evidence = pl.pallas_call(
        hand_over,
        out_shape=(
            jax.ShapeDtypeStruct(coefficients.shape, f32),
            jax.ShapeDtypeStruct(evidence.shape, f32),
        ),
        in_specs=[vmem, vmem],
        out_specs=(vmem, vmem),
    )(coefficients, evidence)
    coefficients = jnp.transpose(coefficients).reshape(rows_out, 2, shells)
    return (coefficients, evidence.reshape(dev_images))


def solution(mesh):
    in_specs = (
        P(None, "shell", "ang", ("grp", "rot")),
        P(None, "shell", "ang", ("grp", "rot")),
        P(("grp", "shell")),
        P(None, ("grp", "rot")),
        P(("grp", "rot"), None),
        P(("grp", "rot"), None, None),
        P(("grp", "rot")),
    )
    out_specs = (P(("grp", "rot", "ang"), None, "shell"), P(("grp", "rot")))
    return jax.shard_map(
        per_device, mesh=mesh, in_specs=in_specs, out_specs=out_specs, check_vma=False
    )
```

```python
import functools
import math

import jax
import jax.numpy as jnp
import numpy as np
from jax import lax
from jax.experimental import pallas as pl
from jax.experimental.pallas import tpu as pltpu
from jax.sharding import PartitionSpec as P

ANGLES = 64
ORDER = 32
BLOCK = 128
CPO = 8
COEF = 1024
HALF = 16
LANES = 128
CHUNK = 256
MESH = pl.DeviceIdType.MESH


def legendre_constants(degrees):
    table = np.zeros((degrees, 2 * degrees), np.float32)
    diagonal = []
    running = 1.0
    for degree in range(degrees):
        for azimuth in range(degree):
            table[azimuth, degree] = math.sqrt(
                (4.0 * degree * degree - 1.0) / (degree * degree - azimuth * azimuth)
            )
            lower_term = max((degree - 1.0) ** 2 - azimuth * azimuth, 0.0)
            lower_den = max(4.0 * (degree - 1.0) ** 2 - 1.0, 1.0)
            table[azimuth, degrees + degree] = math.sqrt(lower_term / lower_den)
        if degree > 0:
            running = running * (2.0 * degree - 1.0) / (2.0 * degree)
        diagonal.append(math.sqrt((2.0 * degree + 1.0) / (4.0 * math.pi) * running))
    return table, diagonal


def nt_dot(left, right):
    return lax.dot_general(
        left, right, (((1,), (1,)), ((), ())), preferred_element_type=jnp.float32
    )


def kernel(
    sizes,
    diagonal,
    images,
    images_again,
    references,
    weight_in,
    count_in,
    rotation_in,
    euler_in,
    order_in,
    constants_in,
    out,
    evidence_out,
    image_buf,
    angle_buf,
    ref_buf,
    native,
    by_angle,
    weight_row,
    counts,
    rotations,
    euler,
    order,
    constants,
    weight_tile,
    requests,
    slot_block,
    wanted,
    eulers,
    slices,
    shares,
    dir_rows,
    cos_rows,
    sin_rows,
    table,
    averages,
    ordered,
    coef,
    ang_recv,
    rot_send,
    rot_recv,
    load_sem,
    req_sem,
    eul_sem,
    slice_sem,
    share_sem,
    ang_sem,
    rot_sem,
    turn_sem,
):
    owners, shell_size, ang_size, shells, angles, rots = sizes
    half = shells * angles
    cs = 2 * shells
    slots = owners * CPO
    dirs = slots * angles
    rows_out = COEF // (owners * ang_size)
    dev_images = order.shape[1]
    columns = dev_images // LANES
    blocks = counts.shape[0]
    rot = lax.axis_index("rot")
    shell = lax.axis_index("shell")
    ang = lax.axis_index("ang")
    sharers = shell_size * ang_size
    lin = shell * ang_size + ang

    loads = []

    def load(src, dst):
        copy = pltpu.make_async_copy(src, dst, load_sem.at[len(loads)])
        copy.start()
        loads.append(copy)

    load(count_in, counts)
    load(rotation_in, rotations)
    load(euler_in, euler)
    load(weight_in, weight_row)
    load(order_in, order)
    load(constants_in, constants)
    load(references, ref_buf)
    for h in range(columns):
        load(images.at[:, h * LANES : (h + 1) * LANES], image_buf.at[h])

    hops = sorted(range(1, owners), key=lambda k: abs(2 * k - owners))
    rot_ids = [{"rot": lax.rem(rot + k, owners)} for k in hops]
    share_ids = []
    for k in range(1, sharers):
        other = lax.rem(lin + k, sharers)
        share_ids.append({"shell": other // ang_size, "ang": lax.rem(other, ang_size)})
    barrier = pltpu.get_barrier_semaphore()
    for device in rot_ids + share_ids:
        pl.semaphore_signal(barrier, inc=1, device_id=device, device_id_type=MESH)

    def send(src, dst, sems, device):
        copy = pltpu.make_async_remote_copy(
            src_ref=src,
            dst_ref=dst,
            send_sem=sems[0],
            recv_sem=sems[1],
            device_id=device,
            device_id_type=MESH,
        )
        copy.start()
        return copy

    for copy in loads[:3]:
        copy.wait()
    place = lax.broadcasted_iota(jnp.int32, (CPO, CPO), 0).astype(jnp.float32)
    entry = lax.broadcasted_iota(jnp.int32, (CPO, CPO), 1).astype(jnp.float32)
    for owner in range(owners):
        local = place
        rotation = jnp.zeros((CPO, 1), jnp.float32)
        block = jnp.full((CPO, CPO), -1.0, jnp.float32)
        for b in range(blocks):
            count = counts[b : b + 1, owner : owner + 1].astype(jnp.float32)
            listed = rotations[b][owner : owner + 1, :].astype(jnp.float32)
            inside = (local >= 0.0) & (local < count)
            rotation += jnp.sum(
                jnp.where(inside & (local == entry), listed, 0.0), axis=1, keepdims=True
            )
            block = jnp.where(inside, float(b), block)
            local = local - count
        requests[owner] = jnp.broadcast_to(rotation, (CPO, LANES)).astype(jnp.int32)
        slot_block[owner * CPO : (owner + 1) * CPO, :] = jnp.broadcast_to(
            block[:, :1], (CPO, LANES)
        )
    wanted[rot] = requests[rot]
    eulers[rot] = euler[...]

    pl.semaphore_wait(barrier, len(rot_ids) + len(share_ids))
    sent = []
    small = []
    for k, device in enumerate(rot_ids):
        small.append(
            send(requests.at[device["rot"]], wanted.at[rot],
                 (req_sem.at[0, k], req_sem.at[1, k]), device)
        )
    late = []
    for k, device in enumerate(rot_ids):
        late.append(send(euler, eulers.at[rot], (eul_sem.at[0, k], eul_sem.at[1, k]), device))

    loads[3].wait()
    diag = lax.broadcasted_iota(jnp.int32, (shells, shells), 0) == lax.broadcasted_iota(
        jnp.int32, (shells, shells), 1
    )
    weight_col = jnp.sum(jnp.where(diag, weight_row[...], 0.0), axis=1, keepdims=True)
    weight_tile[...] = jnp.broadcast_to(weight_col, (shells, LANES))
    shell_at = lax.broadcasted_iota(jnp.int32, (shells, half), 0) * angles
    lane_at = lax.broadcasted_iota(jnp.int32, (shells, half), 1)
    spread = (lane_at >= shell_at) & (lane_at < shell_at + angles)
    weight_lanes = jnp.sum(jnp.where(spread, weight_col, 0.0), axis=0, keepdims=True)

    for copy in loads[7:]:
        copy.wait()

    def weigh(s, carry):
        scale = weight_tile[pl.ds(s, 1), :]
        for part in range(2):
            at = pl.ds(pl.multiple_of(part * half + s * angles, angles), angles)
            for h in range(columns):
                native[at, h * LANES : (h + 1) * LANES] = (image_buf[h, at, :] * scale).astype(
                    jnp.bfloat16
                )
        return carry

    step = min(half, 512)
    pieces = half // step
    early_shells = step // angles
    lax.fori_loop(0, early_shells, weigh, 0, unroll=4)

    for copy in small:
        copy.wait_recv()
    sent += small
    loads[6].wait()
    ids = wanted[...].reshape(slots, LANES)[:, :1]
    selector = (ids == lax.broadcasted_iota(jnp.int32, (slots, rots), 1)).astype(jnp.float32)
    selector = selector.astype(jnp.bfloat16)
    moving = []
    for piece in range(pieces):
        start = piece * step
        low = nt_dot(selector, ref_buf[start : start + step, :])
        high = nt_dot(selector, ref_buf[half + start : half + start + step, :])
        for owner in range(owners):
            at = slice(owner * CPO, (owner + 1) * CPO)
            slices[owner, :, start : start + step] = jnp.concatenate(
                [low[at], high[at]], axis=0
            ).astype(jnp.bfloat16)
        line = []
        for k, device in enumerate(rot_ids):
            line.append(
                send(
                    slices.at[device["rot"], :, start : start + step],
                    slices.at[owners + rot, :, start : start + step],
                    (slice_sem.at[0, piece, k], slice_sem.at[1, piece, k]),
                    device,
                )
            )
        moving.append(line)
    slices[owners + rot] = slices[rot]

    by_turn = []
    for a in range(angles):
        by_turn.append(
            pltpu.make_async_copy(images_again.at[:, a], angle_buf.at[a], turn_sem.at[a])
        )
        by_turn[-1].start()

    lax.fori_loop(early_shells, shells, weigh, 0, unroll=4)

    loads[4].wait()
    member = order[...] == lax.broadcasted_iota(jnp.int32, (dev_images, dev_images), 0)
    member = member.astype(jnp.float32).astype(jnp.bfloat16)
    position = lax.broadcasted_iota(jnp.int32, (8, dev_images), 1)
    block_of = jnp.zeros((8, dev_images), jnp.float32)
    for b in range(1, blocks):
        block_of = jnp.where(position >= b * BLOCK, float(b), block_of)
    image_block = nt_dot(block_of.astype(jnp.bfloat16), member)[:1]

    for copy in late:
        copy.wait_recv()
    sent += late
    lane = lax.broadcasted_iota(jnp.int32, (1, dirs), 1).astype(jnp.float32)
    angle = jnp.floor((lane + 0.5) * (1.0 / slots))
    lane_slot = lane - angle * slots
    angle = angle + (ang * angles).astype(jnp.float32)
    rows3 = [jnp.zeros((1, dirs), jnp.float32) for _ in range(3)]
    row_slot = lax.broadcasted_iota(jnp.int32, (CPO, dirs), 0).astype(jnp.float32)
    for owner in range(owners):
        hit = requests[owner][:, :1] == lax.broadcasted_iota(jnp.int32, (CPO, rots), 1)
        here = lane_slot == row_slot + float(owner * CPO)
        for i in range(3):
            value = jnp.sum(
                jnp.where(hit, eulers[owner][i : i + 1, :], 0.0), axis=1, keepdims=True
            )
            rows3[i] += jnp.sum(jnp.where(here, value, 0.0), axis=0, keepdims=True)
    phase = (2.0 * math.pi / ANGLES) * angle + rows3[2]
    stacked = jnp.concatenate([rows3[0], rows3[1], phase], axis=0)
    cosines, sines = jnp.cos(stacked), jnp.sin(stacked)
    cos_a, cos_b, cos_p = cosines[0:1], cosines[1:2], cosines[2:3]
    sin_a, sin_b, sin_p = sines[0:1], sines[1:2], sines[2:3]
    x = cos_a * cos_b * cos_p - sin_a * sin_p
    y = sin_a * cos_b * cos_p + cos_a * sin_p
    dir_rows[...] = -sin_b * cos_p
    real = jnp.ones_like(x)
    imag = jnp.zeros_like(x)
    for m in range(ORDER):
        factor = math.sqrt(2.0) if m else 1.0
        cos_rows[m : m + 1, :] = real * factor
        sin_rows[m : m + 1, :] = imag * factor if m else real
        real, imag = x * real - y * imag, x * imag + y * real

    loads[5].wait()
    width = min(CHUNK, dirs)

    @pl.loop(0, dirs // width)
    def _(turn):
        lanes = pl.ds(pl.multiple_of(turn * width, width), width)
        z = dir_rows[:, lanes]
        prev = jnp.zeros((HALF, width), jnp.float32)
        early = prev
        for degree in range(ORDER):
            rows = HALF if degree < HALF else ORDER
            if degree == HALF:
                pad = jnp.zeros((ORDER - HALF, width), jnp.float32)
                prev = jnp.concatenate([prev, pad], axis=0)
                early = jnp.concatenate([early, pad], axis=0)
            first = constants[:rows, degree : degree + 1]
            second = constants[:rows, ORDER + degree : ORDER + degree + 1]
            now = first * (z * prev - second * early)
            azimuth = lax.broadcasted_iota(jnp.int32, (rows, width), 0)
            now = jnp.where(azimuth == degree, diagonal[degree], now)
            cosine = now * cos_rows[:rows, lanes]
            sine = now * sin_rows[:rows, lanes]
            first_row = degree * degree
            for h in range(width // LANES):
                at = slice(h * LANES, (h + 1) * LANES)
                ordered[h, pl.ds(first_row, degree + 1, stride=2), :] = sine[: degree + 1, at]
                if degree:
                    ordered[h, pl.ds(first_row + 1, degree, stride=2), :] = cosine[
                        1 : degree + 1, at
                    ]
            prev, early = now, prev
        for h in range(width // LANES):
            at = pl.ds(pl.multiple_of(turn * width + h * LANES, LANES), LANES)
            table[:, at] = ordered[h].astype(jnp.bfloat16)

    partial = jnp.zeros((slots, dev_images), jnp.float32)
    for piece in range(pieces):
        for copy in moving[piece]:
            copy.wait_recv()
        sent += moving[piece]
        start = piece * step
        got = slices[owners:, :, start : start + step].reshape(owners * 2 * CPO, step)
        squares = jnp.square(got.astype(jnp.float32)) * weight_lanes[:, start : start + step]
        norms = jnp.sum(squares, axis=1, keepdims=True)
        low = jnp.dot(got, native[start : start + step, :], preferred_element_type=jnp.float32)
        high = jnp.dot(
            got, native[half + start : half + start + step, :], preferred_element_type=jnp.float32
        )
        low = (2.0 * low - norms).reshape(owners, 2, CPO, dev_images)[:, 0]
        high = (2.0 * high - norms).reshape(owners, 2, CPO, dev_images)[:, 1]
        partial = partial + (low + high).reshape(slots, dev_images)
    shares[lin] = partial
    moving = []
    for k, device in enumerate(share_ids):
        moving.append(
            send(shares.at[lin], shares.at[lin], (share_sem.at[0, k], share_sem.at[1, k]), device)
        )
    for copy in by_turn:
        copy.wait()
    for a in range(angles):
        for part in range(2):
            for h in range(columns):
                at = slice(h * LANES, (h + 1) * LANES)
                first = a * cs + part * shells
                by_angle[first : first + shells, at] = (
                    angle_buf[a, part * shells : (part + 1) * shells, at] * weight_tile[...]
                ).astype(jnp.bfloat16)
    for copy in moving:
        copy.wait_recv()
    sent += moving
    scores = shares[0]
    for k in range(1, sharers):
        scores = scores + shares[k]

    valid = slot_block[:, :1] == image_block
    masked = jnp.where(valid, scores, -3.0e38)
    highest = jnp.max(masked, axis=0, keepdims=True)
    total = jnp.sum(jnp.where(valid, jnp.exp(masked - highest), 0.0), axis=0, keepdims=True)
    evidence = highest + jnp.log(total)
    evidence_out[...] = evidence
    weights = jnp.where(valid, jnp.exp(masked - evidence), 0.0).astype(jnp.bfloat16)

    if cs < averages.shape[1]:
        averages[...] = jnp.zeros(averages.shape, jnp.bfloat16)
    per = 2 if cs % LANES == 0 and angles % 2 == 0 else 1
    for a in range(0, angles, per):
        pair = nt_dot(weights, by_angle[a * cs : (a + per) * cs, :]).astype(jnp.bfloat16)
        for i in range(per):
            averages[(a + i) * slots : (a + i + 1) * slots, :cs] = pair[:, i * cs : (i + 1) * cs]

    moving = []
    across = []
    turns = hops + [0]

    def start_along(i):
        total_here = coef[i, ang]
        for k, copy in enumerate(across[i]):
            copy.wait_recv()
            total_here = total_here + ang_recv[k, i]
        if i < owners - 1:
            rot_send[i] = total_here.astype(jnp.bfloat16)
            moving.append(
                send(
                    rot_send.at[i],
                    rot_recv.at[i],
                    (rot_sem.at[0, i], rot_sem.at[1, i]),
                    rot_ids[i],
                )
            )
        return total_here

    group = ang_size * rows_out
    for i, hop in enumerate(turns):
        start = pl.multiple_of(lax.rem(rot + hop, owners) * group, group)
        rows = jnp.dot(
            table[pl.ds(start, group), :], averages[...], preferred_element_type=jnp.float32
        )
        for k in range(ang_size):
            coef[i, k] = rows[k * rows_out : (k + 1) * rows_out]
        line = []
        for k in range(1, ang_size):
            other = lax.rem(ang + k, ang_size)
            line.append(
                send(
                    coef.at[i, other],
                    ang_recv.at[k - 1, i],
                    (ang_sem.at[0, k - 1, i], ang_sem.at[1, k - 1, i]),
                    {"ang": other},
                )
            )
        across.append(line)
        if i:
            start_along(i - 1)
    total_here = start_along(owners - 1)
    for i, copy in enumerate(moving):
        copy.wait_recv()
        total_here = total_here + rot_recv[i].astype(jnp.float32)
    sent += moving
    out[...] = jnp.transpose(total_here)[:cs]
    for copy in sent:
        copy.wait_send()
    for line in across:
        for copy in line:
            copy.wait_send()


def hand_over(coef_in, evidence_in, coef_out, evidence_out):
    coef_out[...] = coef_in[...]
    evidence_out[...] = evidence_in[...]


def per_device(
    images, references, noise_weight, euler_angles, candidate_count, candidate_rotation, image_order
):
    owners = lax.axis_size("rot")
    shell_size = lax.axis_size("shell")
    ang_size = lax.axis_size("ang")
    _, shells, angles, dev_images = images.shape
    rots = references.shape[3]
    features = 2 * shells * angles
    half = shells * angles
    cs = 2 * shells
    slots = owners * CPO
    dirs = slots * angles
    sharers = shell_size * ang_size
    rows_out = COEF // (owners * ang_size)
    wide = max(cs, LANES)

    table, diagonal = legendre_constants(ORDER)
    vmem = pl.BlockSpec(memory_space=pltpu.VMEM)
    hbm = pl.BlockSpec(memory_space=pl.ANY)
    sizes = (owners, shell_size, ang_size, shells, angles, rots)
    f32, bf16 = jnp.float32, jnp.bfloat16
    dma = pltpu.SemaphoreType.DMA
    columns = dev_images // LANES
    blocks = candidate_count.shape[0]
    others = max(owners - 1, 1)
    pieces = half // min(half, 512)
    coefficients, evidence = pl.pallas_call(
        functools.partial(kernel, sizes, diagonal),
        out_shape=(
            jax.ShapeDtypeStruct((cs, rows_out), f32),
            jax.ShapeDtypeStruct((1, dev_images), f32),
        ),
        in_specs=[hbm] * 9,
        out_specs=(vmem, vmem),
        scratch_shapes=[
            pltpu.VMEM((columns, features, LANES), f32),
            pltpu.VMEM((angles, cs, dev_images), f32),
            pltpu.VMEM((features, rots), bf16),
            pltpu.VMEM((features, dev_images), bf16),
            pltpu.VMEM((features, dev_images), bf16),
            pltpu.VMEM((1, shells), f32),
            pltpu.VMEM((blocks, owners), jnp.int32),
            pltpu.VMEM((blocks, owners, CPO), jnp.int32),
            pltpu.VMEM((3, rots), f32),
            pltpu.VMEM((1, dev_images), jnp.int32),
            pltpu.VMEM(table.shape, f32),
            pltpu.VMEM((shells, LANES), f32),
            pltpu.VMEM((owners, CPO, LANES), jnp.int32),
            pltpu.VMEM((slots, LANES), f32),
            pltpu.VMEM((owners, CPO, LANES), jnp.int32),
            pltpu.VMEM((owners, 3, rots), f32),
            pltpu.VMEM((2 * owners, 2 * CPO, half), bf16),
            pltpu.VMEM((sharers, slots, dev_images), f32),
            pltpu.VMEM((1, dirs), f32),
            pltpu.VMEM((ORDER, dirs), f32),
            pltpu.VMEM((ORDER, dirs), f32),
            pltpu.VMEM((COEF, dirs), bf16),
            pltpu.VMEM((dirs, wide), bf16),
            pltpu.VMEM((min(CHUNK, dirs) // LANES, COEF, LANES), f32),
            pltpu.VMEM((owners, ang_size, rows_out, wide), f32),
            pltpu.VMEM((max(ang_size - 1, 1), owners, rows_out, wide), f32),
            pltpu.VMEM((others, rows_out, wide), bf16),
            pltpu.VMEM((others, rows_out, wide), bf16),
            dma((7 + columns,)),
            dma((2, others)),
            dma((2, others)),
            dma((2, pieces, others)),
            dma((2, max(sharers - 1, 1))),
            dma((2, max(ang_size - 1, 1), owners)),
            dma((2, others)),
            dma((angles,)),
        ],
        compiler_params=pltpu.CompilerParams(
            collective_id=0, has_side_effects=True, vmem_limit_bytes=60 * 1024 * 1024
        ),
    )(
        images.reshape(features, dev_images),
        images.reshape(cs, angles, dev_images),
        references.reshape(features, rots),
        noise_weight[None, :],
        candidate_count,
        candidate_rotation,
        euler_angles,
        image_order[None, :],
        jnp.asarray(table),
    )
    coefficients, evidence = pl.pallas_call(
        hand_over,
        out_shape=(
            jax.ShapeDtypeStruct(coefficients.shape, f32),
            jax.ShapeDtypeStruct(evidence.shape, f32),
        ),
        in_specs=[vmem, vmem],
        out_specs=(vmem, vmem),
    )(coefficients, evidence)
    coefficients = jnp.transpose(coefficients).reshape(rows_out, 2, shells)
    return (coefficients, evidence.reshape(dev_images))


def solution(mesh):
    in_specs = (
        P(None, "shell", "ang", ("grp", "rot")),
        P(None, "shell", "ang", ("grp", "rot")),
        P(("grp", "shell")),
        P(None, ("grp", "rot")),
        P(("grp", "rot"), None),
        P(("grp", "rot"), None, None),
        P(("grp", "rot")),
    )
    out_specs = (P(("grp", "rot", "ang"), None, "shell"), P(("grp", "rot")))
    return jax.shard_map(
        per_device, mesh=mesh, in_specs=in_specs, out_specs=out_specs, check_vma=False
    )
```
